32 devices in a mesh: groups: 2 (over y), lon: 4 (over z), chan: 4 (over x, core).
Axes of the slice: x: 2, y: 2, z: 4, core: 2. Of those that a mesh axis runs over, the one named last changes fastest.
Arguments:
- inputs: bfloat16 [2, 16, 8, 512], P(None, None, 'groups', 'lon'), parts along dimension 2, may hold values from -6 to 6
- hidden_init: bfloat16 [256, 8, 512], P('chan', 'groups', 'lon'), parts along dimension 1, may hold values from -0.8984375 to 0.8984375
- cell_init: float32 [256, 8, 512], P('chan', 'groups', 'lon'), parts along dimension 1, may hold values from -6 to 6
- w_input: bfloat16 [5, 5, 1024, 16], P(None, None, 'chan'), may hold values from -0.3125 to 0.3125
- w_hidden: bfloat16 [5, 5, 1024, 256], P(None, None, 'chan'), may hold values from -0.078125 to 0.078125
- gate_bias: float32 [1024], P('chan'), may hold values from -1 to 1
Outputs:
- hidden_out: bfloat16 [256, 8, 512], P('chan', 'groups', 'lon'), parts along dimension 1
- cell_out: float32 [256, 8, 512], P('chan', 'groups', 'lon'), parts along dimension 1
The draws below stay inside these ranges and needn't reach their ends.
There are 2 independent parts, one for each index of `groups`. The reference program is written for one: setup_inputs(seed, part) draws one part's arguments, and reference() takes and returns one part's arrays. A program takes and returns all parts, laid end to end along the dimension named above; an argument that names none is the same for every part. Nothing has to cross between parts.
All inputs are finite; a program needn't handle non-finite values.
Results may differ from the reference program's by a relative error of at most 0.0019.
Values may be sent and summed in bfloat16 or wider, within the bound.
No kernel may reach another device: no remote copies, remote signals or barrier semaphores. Data moves between devices by JAX's collectives and lax.ppermute only.
A program may use at most 64 MiB of HBM per device.

```python
import jax
import jax.numpy as jnp
from jax import lax

C = 256
CIN = 16
KS = 5
STEPS = 2
LAT = 4
NLON = 512
GATES = 1024


def block_levels(key, extent, cuts, low, high):
    def one(axis_at, blocks):
        heights = jax.random.uniform(jax.random.fold_in(jax.random.fold_in(key, 6), axis_at), (blocks,), jnp.float32, low / len(cuts), high / len(cuts))
        return jnp.repeat(jnp.exp(heights), extent[axis_at] // blocks).reshape((-1,) + (1,) * (len(extent) - axis_at - 1))

    factor_of = one(*cuts[0])
    for cut in cuts[1:]:
        factor_of = factor_of * one(*cut)
    return factor_of


def bell_draw(key, extent, scale, reach, pieces=(), kind=jnp.bfloat16):
    entries = scale * jax.random.normal(key, extent, jnp.float32)
    if pieces:
        entries = entries * block_levels(key, extent, pieces, -0.22, 0.18)
    return jnp.clip(entries, -reach, reach).astype(kind)


def setup_inputs(seed: int = 0, part: int = 0) -> dict:
    key_list = jax.random.split(jax.random.key(seed), 7)
    part_keys = jax.random.split(jax.random.fold_in(key_list[6], part), 7)
    return {
        "inputs": bell_draw(part_keys[0], (STEPS, CIN, LAT, NLON), 1.0, 6.0, ((3, 4),)),
        "hidden_init": jnp.clip(jax.random.uniform(part_keys[1], (C, LAT, NLON), jnp.float32, -0.8984375, 0.8984375) * block_levels(part_keys[1], (C, LAT, NLON), ((0, 4), (2, 4)), -0.4, 0.0), -0.8984375, 0.8984375).astype(jnp.bfloat16),
        "cell_init": bell_draw(part_keys[2], (C, LAT, NLON), 1.0, 6.0, ((0, 4), (2, 4)), jnp.float32),
        "w_input": bell_draw(key_list[3], (KS, KS, GATES, CIN), (KS * KS * CIN) ** -0.5, 0.3125, ((2, 4),)),
        "w_hidden": bell_draw(key_list[4], (KS, KS, GATES, C), (KS * KS * C) ** -0.5, 0.078125, ((2, 4),)),
        "gate_bias": jnp.clip(jax.random.uniform(key_list[5], (GATES,), jnp.float32, -1.0, 1.0) * block_levels(key_list[5], (GATES,), ((0, 4),), -0.4, 0.0), -1.0, 1.0),
    }


def convolve(field, weights):
    padded = jnp.pad(field.astype(jnp.float32), ((0, 0), (2, 2), (0, 0)))
    padded = jnp.concatenate([padded[:, :, -2:], padded, padded[:, :, :2]], axis=2)
    result = lax.conv_general_dilated(padded[None], weights.astype(jnp.float32), (1, 1), "VALID", dimension_numbers=("NCHW", "HWOI", "NCHW"), precision=lax.Precision.HIGHEST)
    return result[0]


def reference(inputs, hidden_init, cell_init, w_input, w_hidden, gate_bias):
    hidden = hidden_init
    cell = cell_init
    for step in range(STEPS):
        pre = convolve(inputs[step], w_input) + convolve(hidden, w_hidden) + gate_bias[:, None, None]
        pre = pre.reshape(-1, 4, pre.shape[1], pre.shape[2])
        in_gate = jax.nn.sigmoid(pre[:, 0])
        forget = jax.nn.sigmoid(pre[:, 1])
        update = jnp.tanh(pre[:, 2])
        out_gate = jax.nn.sigmoid(pre[:, 3])
        cell = forget * cell + in_gate * update
        hidden = (out_gate * jnp.tanh(cell)).astype(jnp.bfloat16)
    return hidden, cell
```

```python
import functools

import jax
import jax.numpy as jnp
from jax import lax
from jax.experimental import pallas as pl
from jax.experimental.pallas import tpu as pltpu
from jax.sharding import PartitionSpec as P

STEPS = 2
FOLD = 16
F32, BF16 = jnp.float32, jnp.bfloat16


def lanes(rows):
    return lax.broadcasted_iota(jnp.int32, (rows, 128), 1)


def roll(x, by):
    by = by % 128
    return pltpu.roll(x, by, 1) if by else x


def unfold(block, channels):
    return jnp.concatenate(
        [roll(block[8 * (i // 4) : 8 * (i // 4) + 8], -32 * (i % 4)) for i in range(channels // 8)], axis=0
    )


def fold(field):
    lane = lanes(8)
    parts = [jnp.zeros((8, 128), F32) for _ in range(FOLD // 8)]
    for i in range(field.shape[0] // 8):
        base = 32 * (i % 4)
        here = (lane >= base) & (lane < base + 32)
        parts[i // 4] = jnp.where(here, roll(field[8 * i : 8 * i + 8], base), parts[i // 4])
    return jnp.concatenate(parts, axis=0)


def edges_of(rows, groups, vectors):
    lane = lanes(8)
    left = [jnp.zeros((8, 128), F32) for _ in range(vectors)]
    right = [jnp.zeros((8, 128), F32) for _ in range(vectors)]
    for i in range(groups):
        for y in range(4):
            base = 32 * (i % 4) + 8 * y
            moved = roll(rows(i, y), base + 4)
            left[i // 4] = jnp.where((lane >= base + 4) & (lane < base + 8), moved, left[i // 4])
            right[i // 4] = jnp.where((lane >= base) & (lane < base + 4), moved, right[i // 4])
    return jnp.concatenate(left, axis=0), jnp.concatenate(right, axis=0)


def pack_kernel(hid, cell, inp, to_left, to_right, main, hid32, inp32):
    ch = hid.shape[0] // 4
    hid32[...] = hid[...].astype(F32)
    inp32[...] = inp[...].astype(F32)
    hl, hr = edges_of(lambda i, y: hid32[pl.ds(32 * i + y, 8, stride=4), :], ch // 8, 2)
    cl, cr = edges_of(lambda i, y: cell[pl.ds(32 * i + y, 8, stride=4), :], ch // 8, 2)
    il, ir = edges_of(lambda i, y: inp32[pl.ds(32 * i + y, 8, stride=4), :], inp.shape[0] // 32, 1)
    to_left[0:FOLD] = hl + roll(cl, -4)
    to_left[FOLD:] = il
    to_right[0:FOLD] = hr + roll(cr, 4)
    to_right[FOLD:] = ir
    for y in range(4):
        main[y * ch : (y + 1) * ch, :] = hid32[pl.ds(y, ch, stride=4), :].astype(BF16)


def join_kernel(main, from_left, from_right, out):
    n = main.shape[0]
    out[0:n] = main[...]
    low = (lanes(FOLD) & 7) < 4
    out[n : n + FOLD] = jnp.where(low, from_left[0:FOLD], from_right[0:FOLD]).astype(BF16)


def windows(row, halo, y):
    lane = lanes(row.shape[0])
    ring = roll(halo, -(8 * y + 4))
    out = []
    for d in range(-2, 3):
        if d == 0:
            out.append(row)
        else:
            other = lane >= 128 + d if d < 0 else lane < d
            out.append(roll(jnp.where(other, ring, row), -d))
    return out


def strips(rows, halo):
    lane = lanes(halo.shape[0])
    low, left = (lane & 7) < 4, lane < 64
    own = jnp.zeros_like(halo)
    for y in range(4):
        here = (lane >= 8 * y + 16) & (lane < 8 * y + 24)
        own = jnp.where(here, roll(rows[y], 8 * y + 20), own)
    rim = jnp.where(lane < 32, halo, jnp.zeros_like(halo))
    return jnp.where(
        left, jnp.where(low, roll(rim, 16), own), jnp.where(low, roll(own, 64), roll(rim, 80))
    )


def sigmoid(x):
    return 0.5 * jnp.tanh(0.5 * x) + 0.5


def gates(pre, ch, at, cell):
    part = [pre[at, pl.ds(g, ch, stride=4), :] for g in range(4)]
    cell = sigmoid(part[1]) * cell + sigmoid(part[0]) * jnp.tanh(part[2])
    return sigmoid(part[3]) * jnp.tanh(cell), cell


def step_kernel(step, *refs):
    last = step == STEPS - 1
    gathered, from_left, from_right, inp, cell, w, wx, bias = refs[:8]
    hid_out, cell_out, xs, xi, wxb, pre, inp32 = refs[8:15]
    shards, ch = gathered.shape[0], (gathered.shape[1] - FOLD) // 4
    depth, cin = shards * ch, inp.shape[0] // (4 * STEPS)
    taps = 25 * cin
    rows = [
        jnp.concatenate([gathered[c, y * ch : (y + 1) * ch, :] for c in range(shards)], axis=0) for y in range(4)
    ]
    halo = jnp.concatenate(
        [unfold(gathered[c, 4 * ch : 4 * ch + FOLD, :].astype(F32), ch) for c in range(shards)], axis=0
    ).astype(BF16)
    for b in range(5):
        xs[b, :, 0:128] = jnp.zeros((depth, 128), BF16)
        xs[b, :, 640:768] = jnp.zeros((depth, 128), BF16)
    for y in range(4):
        for b, window in enumerate(windows(rows[y], halo, y)):
            xs[b, :, 128 * (y + 1) : 128 * (y + 2)] = window
    inp32[...] = inp[...].astype(F32)
    irows = [inp32[pl.ds(4 * cin * step + y, cin, stride=4), :].astype(BF16) for y in range(4)]
    low = (lanes(8) & 7) < 4
    iblock = jnp.where(low, from_left[FOLD:], from_right[FOLD:])
    first = step * cin // 8
    ihalo = jnp.concatenate([roll(iblock, -32 * i) for i in range(first, first + cin // 8)], axis=0).astype(BF16)
    iwin = [windows(irows[y], ihalo, y) for y in range(4)]
    for a in range(5):
        for b in range(5):
            at = cin * (5 * a + b)
            for y in range(4):
                r = y + a - 2
                xi[at : at + cin, 128 * y : 128 * (y + 1)] = (
                    iwin[r][b] if 0 <= r < 4 else jnp.zeros((cin, 128), BF16)
                )
    count = xi.shape[1]
    ones = lax.broadcasted_iota(jnp.int32, (16, count), 0) < 3
    xi[taps : taps + 16, :] = jnp.where(ones, 1.0, 0.0).astype(BF16)
    wxb[0:taps, :] = wx[...]
    b0 = bias[...]
    b1 = b0.astype(BF16).astype(F32)
    b2 = (b0 - b1).astype(BF16).astype(F32)
    b3 = b0 - b1 - b2
    sub = lax.broadcasted_iota(jnp.int32, (16, wxb.shape[1]), 0)
    wxb[taps : taps + 16, :] = jnp.where(
        sub == 0, b1, jnp.where(sub == 1, b2, jnp.where(sub == 2, b3, 0.0))
    ).astype(BF16)
    if not last:
        istrip = strips(irows, ihalo)
        for a in range(5):
            for b in range(5):
                at = cin * (5 * a + b)
                xi[at : at + cin, 512:640] = roll(istrip, -(8 * (a - 2) + b - 2))
    drive = (((0,), (0,)), ((), ()))
    for pair in range(2):
        terms = [(a, b, 2 * pair + a - 2) for a in range(5) for b in range(5) if -2 < 2 * pair + a - 2 < 4]
        left = jnp.concatenate([w[a, b] for a, b, _ in terms], axis=1)
        right = jnp.concatenate([xs[b, :, 128 * (lo + 1) : 128 * (lo + 3)] for _, b, lo in terms], axis=0)
        at = 256 * pair
        total = jnp.dot(left, right, preferred_element_type=F32) + lax.dot_general(
            wxb[...], xi[:, at : at + 256], drive, preferred_element_type=F32
        )
        pre[2 * pair] = total[:, 0:128]
        pre[2 * pair + 1] = total[:, 128:256]
    for y in range(4):
        before = cell[pl.ds(y, ch, stride=4), :] if step == 0 else cell[y * ch : (y + 1) * ch, :]
        h, c = gates(pre, ch, y, before)
        if last:
            cell_out[pl.ds(y, ch, stride=4), :] = c
            refs[15][pl.ds(y, ch, stride=4), :] = h
        else:
            cell_out[y * ch : (y + 1) * ch, :] = c
            hid_out[y * ch : (y + 1) * ch, :] = h.astype(BF16)
    if last:
        hid_out[...] = refs[15][...].astype(BF16)
        return
    strip = strips(rows, halo)
    stack = jnp.concatenate([roll(strip, -8 * (a - 2)) for a in range(5)], axis=0)
    total = lax.dot_general(wxb[...], xi[:, 512:640], drive, preferred_element_type=F32)
    for b in range(5):
        left = jnp.concatenate([w[a, b] for a in range(5)], axis=1)
        total = total + roll(jnp.dot(left, stack, preferred_element_type=F32), -(b - 2))
    pre[4] = total
    lane = lanes(ch)
    near = lane < 64
    cells = unfold(jnp.where((lanes(FOLD) & 7) < 4, from_right[0:FOLD], from_left[0:FOLD]), ch)
    h, _ = gates(pre, ch, 4, jnp.where(near, roll(cells, 12), roll(cells, 84)))
    h = jnp.where((lane & 7) < 4, roll(h, -16), roll(h, -80))
    hid_out[4 * ch : 4 * ch + FOLD, :] = fold(h).astype(BF16)


def call(kernel, outs, scratch, *args):
    return pl.pallas_call(
        kernel,
        out_shape=[jax.ShapeDtypeStruct(s, d) for s, d in outs],
        in_specs=[pl.BlockSpec(memory_space=pltpu.VMEM)] * len(args),
        out_specs=[pl.BlockSpec(memory_space=pltpu.VMEM)] * len(outs),
        scratch_shapes=[pltpu.VMEM(s, d) for s, d in scratch],
        compiler_params=pltpu.CompilerParams(vmem_limit_bytes=24 << 20),
    )(*args)


def shards(inputs, hidden_init, cell_init, w_input, w_hidden, gate_bias):
    ch, rows, cols = hidden_init.shape
    gate = 4 * ch
    depth = w_hidden.shape[3]
    cin = w_input.shape[3]
    hid = hidden_init.reshape(ch * rows, cols)
    cell = cell_init.reshape(ch * rows, cols)
    inp = inputs.reshape(-1, cols)
    wx = jnp.transpose(w_input, (0, 1, 3, 2)).reshape(25 * cin, gate)
    bias = gate_bias.reshape(1, gate)
    to_left, to_right, main = call(
        pack_kernel,
        [((FOLD + 8, 128), F32), ((FOLD + 8, 128), F32), ((4 * ch, 128), BF16)],
        [((4 * ch, 128), F32), (inp.shape, F32)],
        hid, cell, inp,
    )
    n = lax.axis_size("lon")
    from_right = lax.ppermute(to_left, "lon", [((i + 1) % n, i) for i in range(n)])
    from_left = lax.ppermute(to_right, "lon", [(i, (i + 1) % n) for i in range(n)])
    (field,) = call(join_kernel, [((4 * ch + FOLD, 128), BF16)], [], main, from_left, from_right)
    for step in range(STEPS):
        last = step == STEPS - 1
        gathered = lax.all_gather(field, "chan", axis=0)
        wide = 512 if last else 640
        scratch = [
            ((5, depth, 768), BF16),
            ((25 * cin + 16, wide), BF16),
            ((25 * cin + 16, gate), BF16),
            ((wide // 128, gate, 128), F32),
            (inp.shape, F32),
        ]
        if last:
            scratch.append(((4 * ch, 128), F32))
        field, cell = call(
            functools.partial(step_kernel, step),
            [((4 * ch + (0 if last else FOLD), 128), BF16), ((4 * ch, 128), F32)],
            scratch,
            gathered, from_left, from_right, inp, cell, w_hidden, wx, bias,
        )
    return field.reshape(ch, rows, cols), cell.reshape(ch, rows, cols)


def solution(mesh):
    in_specs = (
        P(None, None, "groups", "lon"),
        P("chan", "groups", "lon"),
        P("chan", "groups", "lon"),
        P(None, None, "chan", None),
        P(None, None, "chan", None),
        P("chan"),
    )
    out_specs = (P("chan", "groups", "lon"), P("chan", "groups", "lon"))
    return jax.shard_map(shards, mesh=mesh, in_specs=in_specs, out_specs=out_specs, check_vma=False)
```

```python
import functools

import jax
import jax.numpy as jnp
from jax import lax
from jax.experimental import pallas as pl
from jax.experimental.pallas import tpu as pltpu
from jax.sharding import PartitionSpec as P

STEPS = 2
FOLD = 16
F32, BF16 = jnp.float32, jnp.bfloat16


def lanes(rows):
    return lax.broadcasted_iota(jnp.int32, (rows, 128), 1)


def roll(x, by):
    by = by % 128
    return pltpu.roll(x, by, 1) if by else x


def unfold(block, channels):
    return jnp.concatenate(
        [roll(block[8 * (i // 4) : 8 * (i // 4) + 8], -32 * (i % 4)) for i in range(channels // 8)], axis=0
    )


def fold(field):
    lane = lanes(8)
    parts = [jnp.zeros((8, 128), F32) for _ in range(FOLD // 8)]
    for i in range(field.shape[0] // 8):
        base = 32 * (i % 4)
        here = (lane >= base) & (lane < base + 32)
        parts[i // 4] = jnp.where(here, roll(field[8 * i : 8 * i + 8], base), parts[i // 4])
    return jnp.concatenate(parts, axis=0)


def edges_of(rows, groups, vectors):
    lane = lanes(8)
    left = [jnp.zeros((8, 128), F32) for _ in range(vectors)]
    right = [jnp.zeros((8, 128), F32) for _ in range(vectors)]
    for i in range(groups):
        for y in range(4):
            base = 32 * (i % 4) + 8 * y
            moved = roll(rows(i, y), base + 4)
            left[i // 4] = jnp.where((lane >= base + 4) & (lane < base + 8), moved, left[i // 4])
            right[i // 4] = jnp.where((lane >= base) & (lane < base + 4), moved, right[i // 4])
    return jnp.concatenate(left, axis=0), jnp.concatenate(right, axis=0)


def pack_kernel(hid_far, cell_far, inp_far, to_left, to_right, main, hid, cell, inp, hid32, inp32, arrived):
    ch = hid.shape[0] // 4
    pairs = ((hid_far, hid), (cell_far, cell), (inp_far, inp))
    copies = [pltpu.make_async_copy(a, b, arrived.at[i]) for i, (a, b) in enumerate(pairs)]
    for copy in copies:
        copy.start()
    for copy in copies:
        copy.wait()
    hid32[...] = hid[...].astype(F32)
    inp32[...] = inp[...].astype(F32)
    hl, hr = edges_of(lambda i, y: hid32[pl.ds(32 * i + y, 8, stride=4), :], ch // 8, 2)
    cl, cr = edges_of(lambda i, y: cell[pl.ds(32 * i + y, 8, stride=4), :], ch // 8, 2)
    il, ir = edges_of(lambda i, y: inp32[pl.ds(32 * i + y, 8, stride=4), :], inp.shape[0] // 32, 1)
    to_left[0:FOLD] = hl + roll(cl, -4)
    to_left[FOLD:] = il
    to_right[0:FOLD] = hr + roll(cr, 4)
    to_right[FOLD:] = ir
    for y in range(4):
        main[y * ch : (y + 1) * ch, :] = hid32[pl.ds(y, ch, stride=4), :].astype(BF16)


def join_kernel(main, from_left, from_right, out):
    n = main.shape[0]
    out[0:n] = main[...]
    low = (lanes(FOLD) & 7) < 4
    out[n : n + FOLD] = jnp.where(low, from_left[0:FOLD], from_right[0:FOLD]).astype(BF16)


def windows(row, halo, y):
    lane = lanes(row.shape[0])
    ring = roll(halo, -(8 * y + 4))
    out = []
    for d in range(-2, 3):
        if d == 0:
            out.append(row)
        else:
            other = lane >= 128 + d if d < 0 else lane < d
            out.append(roll(jnp.where(other, ring, row), -d))
    return out


def strips(rows, halo):
    lane = lanes(halo.shape[0])
    low, left = (lane & 7) < 4, lane < 64
    own = jnp.zeros_like(halo)
    for y in range(4):
        here = (lane >= 8 * y + 16) & (lane < 8 * y + 24)
        own = jnp.where(here, roll(rows[y], 8 * y + 20), own)
    rim = jnp.where(lane < 32, halo, jnp.zeros_like(halo))
    return jnp.where(
        left, jnp.where(low, roll(rim, 16), own), jnp.where(low, roll(own, 64), roll(rim, 80))
    )


def sigmoid(x):
    return 0.5 * jnp.tanh(0.5 * x) + 0.5


def gates(pre, ch, at, cell):
    part = [pre[at, pl.ds(g, ch, stride=4), :] for g in range(4)]
    cell = sigmoid(part[1]) * cell + sigmoid(part[0]) * jnp.tanh(part[2])
    return sigmoid(part[3]) * jnp.tanh(cell), cell


def step_kernel(step, *refs):
    last = step == STEPS - 1
    gathered, from_left, from_right, inp, cell, w, wx, bias = refs[:8]
    hid_out, cell_out, xs, xi, wxb, pre, inp32 = refs[8:15]
    shards, ch = gathered.shape[0], (gathered.shape[1] - FOLD) // 4
    depth, cin = shards * ch, inp.shape[0] // (4 * STEPS)
    taps = 25 * cin
    rows = [
        jnp.concatenate([gathered[c, y * ch : (y + 1) * ch, :] for c in range(shards)], axis=0) for y in range(4)
    ]
    halo = jnp.concatenate(
        [unfold(gathered[c, 4 * ch : 4 * ch + FOLD, :].astype(F32), ch) for c in range(shards)], axis=0
    ).astype(BF16)
    for b in range(5):
        xs[b, :, 0:128] = jnp.zeros((depth, 128), BF16)
        xs[b, :, 640:768] = jnp.zeros((depth, 128), BF16)
    for y in range(4):
        for b, window in enumerate(windows(rows[y], halo, y)):
            xs[b, :, 128 * (y + 1) : 128 * (y + 2)] = window
    inp32[...] = inp[...].astype(F32)
    irows = [inp32[pl.ds(4 * cin * step + y, cin, stride=4), :].astype(BF16) for y in range(4)]
    low = (lanes(8) & 7) < 4
    iblock = jnp.where(low, from_left[FOLD:], from_right[FOLD:])
    first = step * cin // 8
    ihalo = jnp.concatenate([roll(iblock, -32 * i) for i in range(first, first + cin // 8)], axis=0).astype(BF16)
    iwin = [windows(irows[y], ihalo, y) for y in range(4)]
    for a in range(5):
        for b in range(5):
            at = cin * (5 * a + b)
            for y in range(4):
                r = y + a - 2
                xi[at : at + cin, 128 * y : 128 * (y + 1)] = (
                    iwin[r][b] if 0 <= r < 4 else jnp.zeros((cin, 128), BF16)
                )
    count = xi.shape[1]
    ones = lax.broadcasted_iota(jnp.int32, (16, count), 0) < 3
    xi[taps : taps + 16, :] = jnp.where(ones, 1.0, 0.0).astype(BF16)
    wxb[0:taps, :] = wx[...]
    b0 = bias[...]
    b1 = b0.astype(BF16).astype(F32)
    b2 = (b0 - b1).astype(BF16).astype(F32)
    b3 = b0 - b1 - b2
    sub = lax.broadcasted_iota(jnp.int32, (16, wxb.shape[1]), 0)
    wxb[taps : taps + 16, :] = jnp.where(
        sub == 0, b1, jnp.where(sub == 1, b2, jnp.where(sub == 2, b3, 0.0))
    ).astype(BF16)
    if not last:
        istrip = strips(irows, ihalo)
        for a in range(5):
            for b in range(5):
                at = cin * (5 * a + b)
                xi[at : at + cin, 512:640] = roll(istrip, -(8 * (a - 2) + b - 2))
    drive = (((0,), (0,)), ((), ()))
    for pair in range(2):
        terms = [(a, b, 2 * pair + a - 2) for a in range(5) for b in range(5) if -2 < 2 * pair + a - 2 < 4]
        left = jnp.concatenate([w[a, b] for a, b, _ in terms], axis=1)
        right = jnp.concatenate([xs[b, :, 128 * (lo + 1) : 128 * (lo + 3)] for _, b, lo in terms], axis=0)
        at = 256 * pair
        total = jnp.dot(left, right, preferred_element_type=F32) + lax.dot_general(
            wxb[...], xi[:, at : at + 256], drive, preferred_element_type=F32
        )
        pre[2 * pair] = total[:, 0:128]
        pre[2 * pair + 1] = total[:, 128:256]
    for y in range(4):
        before = cell[pl.ds(y, ch, stride=4), :] if step == 0 else cell[y * ch : (y + 1) * ch, :]
        h, c = gates(pre, ch, y, before)
        if last:
            cell_out[pl.ds(y, ch, stride=4), :] = c
            refs[15][pl.ds(y, ch, stride=4), :] = h
        else:
            cell_out[y * ch : (y + 1) * ch, :] = c
            hid_out[y * ch : (y + 1) * ch, :] = h.astype(BF16)
    if last:
        hid_out[...] = refs[15][...].astype(BF16)
        return
    strip = strips(rows, halo)
    stack = jnp.concatenate([roll(strip, -8 * (a - 2)) for a in range(5)], axis=0)
    total = lax.dot_general(wxb[...], xi[:, 512:640], drive, preferred_element_type=F32)
    for b in range(5):
        left = jnp.concatenate([w[a, b] for a in range(5)], axis=1)
        total = total + roll(jnp.dot(left, stack, preferred_element_type=F32), -(b - 2))
    pre[4] = total
    lane = lanes(ch)
    near = lane < 64
    cells = unfold(jnp.where((lanes(FOLD) & 7) < 4, from_right[0:FOLD], from_left[0:FOLD]), ch)
    h, _ = gates(pre, ch, 4, jnp.where(near, roll(cells, 12), roll(cells, 84)))
    h = jnp.where((lane & 7) < 4, roll(h, -16), roll(h, -80))
    hid_out[4 * ch : 4 * ch + FOLD, :] = fold(h).astype(BF16)


def call(kernel, outs, scratch, *args, far=0, us=1):
    return pl.pallas_call(
        kernel,
        out_shape=[jax.ShapeDtypeStruct(s, d) for s, d in outs],
        in_specs=[pl.BlockSpec(memory_space=pltpu.HBM)] * far
        + [pl.BlockSpec(memory_space=pltpu.VMEM)] * (len(args) - far),
        out_specs=[pl.BlockSpec(memory_space=pltpu.VMEM)] * len(outs),
        scratch_shapes=[pltpu.VMEM(s, d) for s, d in scratch] + ([pltpu.SemaphoreType.DMA((far,))] if far else []),
        cost_estimate=pl.CostEstimate(flops=int(us * 1e9), bytes_accessed=0, transcendentals=0),
        compiler_params=pltpu.CompilerParams(vmem_limit_bytes=24 << 20),
    )(*[pltpu.with_memory_space_constraint(a, pltpu.HBM) if i < far else a for i, a in enumerate(args)])


def shards(inputs, hidden_init, cell_init, w_input, w_hidden, gate_bias):
    ch, rows, cols = hidden_init.shape
    gate = 4 * ch
    depth = w_hidden.shape[3]
    cin = w_input.shape[3]
    hid = hidden_init.reshape(ch * rows, cols)
    cell = cell_init.reshape(ch * rows, cols)
    inp = inputs.reshape(-1, cols)
    wx = jnp.transpose(w_input, (0, 1, 3, 2)).reshape(25 * cin, gate)
    bias = gate_bias.reshape(1, gate)
    to_left, to_right, main = call(
        pack_kernel,
        [((FOLD + 8, 128), F32), ((FOLD + 8, 128), F32), ((4 * ch, 128), BF16)],
        [(hid.shape, BF16), (cell.shape, F32), (inp.shape, BF16), (hid.shape, F32), (inp.shape, F32)],
        hid, cell, inp, far=3, us=1,
    )
    n = lax.axis_size("lon")
    from_right = lax.ppermute(to_left, "lon", [((i + 1) % n, i) for i in range(n)])
    from_left = lax.ppermute(to_right, "lon", [(i, (i + 1) % n) for i in range(n)])
    (field,) = call(join_kernel, [((4 * ch + FOLD, 128), BF16)], [], main, from_left, from_right)
    for step in range(STEPS):
        last = step == STEPS - 1
        gathered = lax.all_gather(field, "chan", axis=0)
        wide = 512 if last else 640
        scratch = [
            ((5, depth, 768), BF16),
            ((25 * cin + 16, wide), BF16),
            ((25 * cin + 16, gate), BF16),
            ((wide // 128, gate, 128), F32),
            (inp.shape, F32),
        ]
        if last:
            scratch.append(((4 * ch, 128), F32))
        field, cell = call(
            functools.partial(step_kernel, step),
            [((4 * ch + (0 if last else FOLD), 128), BF16), ((4 * ch, 128), F32)],
            scratch,
            gathered, from_left, from_right, inp, cell, w_hidden, wx, bias, us=3,
        )
    return field.reshape(ch, rows, cols), cell.reshape(ch, rows, cols)


def solution(mesh):
    in_specs = (
        P(None, None, "groups", "lon"),
        P("chan", "groups", "lon"),
        P("chan", "groups", "lon"),
        P(None, None, "chan", None),
        P(None, None, "chan", None),
        P("chan"),
    )
    out_specs = (P("chan", "groups", "lon"), P("chan", "groups", "lon"))
    return jax.shard_map(shards, mesh=mesh, in_specs=in_specs, out_specs=out_specs, check_vma=False)
```

```python
import functools

import jax
import jax.numpy as jnp
from jax import lax
from jax.experimental import pallas as pl
from jax.experimental.pallas import tpu as pltpu
from jax.sharding import PartitionSpec as P

STEPS = 2
FOLD = 16
F32, BF16 = jnp.float32, jnp.bfloat16


def lanes(rows):
    return lax.broadcasted_iota(jnp.int32, (rows, 128), 1)


def roll(x, by):
    by = by % 128
    return pltpu.roll(x, by, 1) if by else x


def unfold(block, channels):
    return jnp.concatenate(
        [roll(block[8 * (i // 4) : 8 * (i // 4) + 8], -32 * (i % 4)) for i in range(channels // 8)], axis=0
    )


def fold(field):
    lane = lanes(8)
    parts = [jnp.zeros((8, 128), F32) for _ in range(FOLD // 8)]
    for i in range(field.shape[0] // 8):
        base = 32 * (i % 4)
        here = (lane >= base) & (lane < base + 32)
        parts[i // 4] = jnp.where(here, roll(field[8 * i : 8 * i + 8], base), parts[i // 4])
    return jnp.concatenate(parts, axis=0)


def edges_of(rows, groups, vectors):
    lane = lanes(8)
    left = [jnp.zeros((8, 128), F32) for _ in range(vectors)]
    right = [jnp.zeros((8, 128), F32) for _ in range(vectors)]
    for i in range(groups):
        for y in range(4):
            base = 32 * (i % 4) + 8 * y
            moved = roll(rows(i, y), base + 4)
            left[i // 4] = jnp.where((lane >= base + 4) & (lane < base + 8), moved, left[i // 4])
            right[i // 4] = jnp.where((lane >= base) & (lane < base + 4), moved, right[i // 4])
    return jnp.concatenate(left, axis=0), jnp.concatenate(right, axis=0)


def pack_kernel(hid_far, cell_far, inp_far, to_left, to_right, main, hid, cell, inp, hid32, inp32, arrived):
    ch = hid.shape[0] // 4
    pairs = ((hid_far, hid), (cell_far, cell), (inp_far, inp))
    copies = [pltpu.make_async_copy(a, b, arrived.at[i]) for i, (a, b) in enumerate(pairs)]
    for copy in copies:
        copy.start()
    for copy in copies:
        copy.wait()
    hid32[...] = hid[...].astype(F32)
    inp32[...] = inp[...].astype(F32)
    hl, hr = edges_of(lambda i, y: hid32[pl.ds(32 * i + y, 8, stride=4), :], ch // 8, 2)
    cl, cr = edges_of(lambda i, y: cell[pl.ds(32 * i + y, 8, stride=4), :], ch // 8, 2)
    il, ir = edges_of(lambda i, y: inp32[pl.ds(32 * i + y, 8, stride=4), :], inp.shape[0] // 32, 1)
    to_left[0:FOLD] = hl + roll(cl, -4)
    to_left[FOLD:] = il
    to_right[0:FOLD] = hr + roll(cr, 4)
    to_right[FOLD:] = ir
    for y in range(4):
        main[y * ch : (y + 1) * ch, :] = hid32[pl.ds(y, ch, stride=4), :].astype(BF16)


def join_kernel(main, from_left, from_right, out):
    n = main.shape[0]
    out[0:n] = main[...]
    low = (lanes(FOLD) & 7) < 4
    out[n : n + FOLD] = jnp.where(low, from_left[0:FOLD], from_right[0:FOLD]).astype(BF16)


def windows(row, halo, y):
    lane = lanes(row.shape[0])
    ring = roll(halo, -(8 * y + 4))
    out = []
    for d in range(-2, 3):
        if d == 0:
            out.append(row)
        else:
            other = lane >= 128 + d if d < 0 else lane < d
            out.append(roll(jnp.where(other, ring, row), -d))
    return out


def strips(rows, halo):
    lane = lanes(halo.shape[0])
    low, left = (lane & 7) < 4, lane < 64
    own = jnp.zeros_like(halo)
    for y in range(4):
        here = (lane >= 8 * y + 16) & (lane < 8 * y + 24)
        own = jnp.where(here, roll(rows[y], 8 * y + 20), own)
    rim = jnp.where(lane < 32, halo, jnp.zeros_like(halo))
    return jnp.where(
        left, jnp.where(low, roll(rim, 16), own), jnp.where(low, roll(own, 64), roll(rim, 80))
    )


def sigmoid(x):
    return 0.5 * jnp.tanh(0.5 * x) + 0.5


def gates(pre, ch, at, cell):
    part = [pre[at, pl.ds(g, ch, stride=4), :] for g in range(4)]
    cell = sigmoid(part[1]) * cell + sigmoid(part[0]) * jnp.tanh(part[2])
    return sigmoid(part[3]) * jnp.tanh(cell), cell


DRIVE = (((0,), (0,)), ((), ()))


def near_far(own, other, ch):
    even = lax.axis_index("chan") % 2 == 0
    low, high = jnp.where(even, own, other), jnp.where(even, other, own)
    return rows_of([low, high], ch)


def rows_of(shards, ch):
    rows = [jnp.concatenate([s[y * ch : (y + 1) * ch] for s in shards], axis=0) for y in range(4)]
    halo = jnp.concatenate([unfold(s[4 * ch : 4 * ch + FOLD].astype(F32), ch) for s in shards], axis=0)
    return rows, halo.astype(BF16)


def store_windows(xs, rows, halo):
    depth = halo.shape[0]
    for b in range(5):
        xs[b, :, 0:128] = jnp.zeros((depth, 128), BF16)
        xs[b, :, 640:768] = jnp.zeros((depth, 128), BF16)
    for y in range(4):
        for b, window in enumerate(windows(rows[y], halo, y)):
            xs[b, :, 128 * (y + 1) : 128 * (y + 2)] = window


def hidden_rows(w, xs, at, pair):
    depth = xs.shape[1]
    terms = [(a, b, 2 * pair + a - 2) for a in range(5) for b in range(5) if -2 < 2 * pair + a - 2 < 4]
    left = jnp.concatenate([w[a, b, :, pl.ds(at, depth)] for a, b, _ in terms], axis=1)
    right = jnp.concatenate([xs[b, :, 128 * (lo + 1) : 128 * (lo + 3)] for _, b, lo in terms], axis=0)
    return jnp.dot(left, right, preferred_element_type=F32)


def hidden_rim(w, rows, halo, at):
    depth = halo.shape[0]
    strip = strips(rows, halo)
    stack = jnp.concatenate([roll(strip, -8 * (a - 2)) for a in range(5)], axis=0)
    total = None
    for b in range(5):
        left = jnp.concatenate([w[a, b, :, pl.ds(at, depth)] for a in range(5)], axis=1)
        part = roll(jnp.dot(left, stack, preferred_element_type=F32), -(b - 2))
        total = part if total is None else total + part
    return total


def store_inputs(step, xi, wxb, inp32, inp, from_left, from_right, wx, bias):
    cin = inp.shape[0] // (4 * STEPS)
    taps = 25 * cin
    inp32[...] = inp[...].astype(F32)
    rows = [inp32[pl.ds(4 * cin * step + y, cin, stride=4), :].astype(BF16) for y in range(4)]
    low = (lanes(8) & 7) < 4
    block = jnp.where(low, from_left[FOLD:], from_right[FOLD:])
    first = step * cin // 8
    halo = jnp.concatenate([roll(block, -32 * i) for i in range(first, first + cin // 8)], axis=0).astype(BF16)
    wins = [windows(rows[y], halo, y) for y in range(4)]
    for a in range(5):
        for b in range(5):
            at = cin * (5 * a + b)
            for y in range(4):
                r = y + a - 2
                xi[at : at + cin, 128 * y : 128 * (y + 1)] = (
                    wins[r][b] if 0 <= r < 4 else jnp.zeros((cin, 128), BF16)
                )
    if xi.shape[1] > 512:
        strip = strips(rows, halo)
        for a in range(5):
            for b in range(5):
                at = cin * (5 * a + b)
                xi[at : at + cin, 512:640] = roll(strip, -(8 * (a - 2) + b - 2))
    ones = lax.broadcasted_iota(jnp.int32, (16, xi.shape[1]), 0) < 3
    xi[taps : taps + 16, :] = jnp.where(ones, 1.0, 0.0).astype(BF16)
    wxb[0:taps, :] = wx[...]
    b0 = bias[...]
    b1 = b0.astype(BF16).astype(F32)
    b2 = (b0 - b1).astype(BF16).astype(F32)
    b3 = b0 - b1 - b2
    sub = lax.broadcasted_iota(jnp.int32, (16, wxb.shape[1]), 0)
    wxb[taps : taps + 16, :] = jnp.where(
        sub == 0, b1, jnp.where(sub == 1, b2, jnp.where(sub == 2, b3, 0.0))
    ).astype(BF16)


def input_part(wxb, xi, at, wide):
    return lax.dot_general(wxb[...], xi[:, at : at + wide], DRIVE, preferred_element_type=F32)


def finish(step, pre, cell, from_left, from_right, hid_out, cell_out, hid32):
    ch = cell.shape[0] // 4
    last = step == STEPS - 1
    for y in range(4):
        before = cell[pl.ds(y, ch, stride=4), :] if step == 0 else cell[y * ch : (y + 1) * ch, :]
        h, c = gates(pre, ch, y, before)
        if last:
            cell_out[pl.ds(y, ch, stride=4), :] = c
            hid32[pl.ds(y, ch, stride=4), :] = h
        else:
            cell_out[y * ch : (y + 1) * ch, :] = c
            hid_out[y * ch : (y + 1) * ch, :] = h.astype(BF16)
    if last:
        hid_out[...] = hid32[...].astype(BF16)
        return
    lane = lanes(ch)
    cells = unfold(jnp.where((lanes(FOLD) & 7) < 4, from_right[0:FOLD], from_left[0:FOLD]), ch)
    h, _ = gates(pre, ch, 4, jnp.where(lane < 64, roll(cells, 12), roll(cells, 84)))
    h = jnp.where((lane & 7) < 4, roll(h, -16), roll(h, -80))
    hid_out[4 * ch : 4 * ch + FOLD, :] = fold(h).astype(BF16)


def whole_kernel(step, gathered, from_left, from_right, inp, cell, w, wx, bias, hid_out, cell_out, xs, xi, wxb, pre, inp32, hid32):
    shards, ch = gathered.shape[0], cell.shape[0] // 4
    rows, halo = rows_of([gathered[c] for c in range(shards)], ch)
    store_windows(xs, rows, halo)
    store_inputs(step, xi, wxb, inp32, inp, from_left, from_right, wx, bias)
    for pair in range(2):
        total = hidden_rows(w, xs, 0, pair) + input_part(wxb, xi, 256 * pair, 256)
        pre[2 * pair] = total[:, 0:128]
        pre[2 * pair + 1] = total[:, 128:256]
    if step < STEPS - 1:
        pre[4] = hidden_rim(w, rows, halo, 0) + input_part(wxb, xi, 512, 128)
    finish(step, pre, cell, from_left, from_right, hid_out, cell_out, hid32)


def first_channel(depth, remote):
    mine = lax.axis_index("chan") // 2
    return pl.multiple_of((1 - mine if remote else mine) * depth, depth)


def near_kernel(step, own, other, from_left, from_right, inp, w, wx, bias, part, xs, xi, wxb, inp32):
    ch = w.shape[2] // 4
    rows, halo = near_far(own[...], other[...], ch)
    at = first_channel(2 * ch, False)
    store_windows(xs, rows, halo)
    store_inputs(step, xi, wxb, inp32, inp, from_left, from_right, wx, bias)
    for pair in range(2):
        total = hidden_rows(w, xs, at, pair) + input_part(wxb, xi, 256 * pair, 256)
        part[2 * pair] = total[:, 0:128]
        part[2 * pair + 1] = total[:, 128:256]
    if step < STEPS - 1:
        part[4] = hidden_rim(w, rows, halo, at) + input_part(wxb, xi, 512, 128)


def far_kernel(step, same, cross, part, from_left, from_right, cell, w, hid_out, cell_out, xs, pre, hid32):
    ch = cell.shape[0] // 4
    rows, halo = near_far(same[...], cross[...], ch)
    at = first_channel(2 * ch, True)
    store_windows(xs, rows, halo)
    for pair in range(2):
        total = hidden_rows(w, xs, at, pair)
        pre[2 * pair] = part[2 * pair] + total[:, 0:128]
        pre[2 * pair + 1] = part[2 * pair + 1] + total[:, 128:256]
    if step < STEPS - 1:
        pre[4] = part[4] + hidden_rim(w, rows, halo, at)
    finish(step, pre, cell, from_left, from_right, hid_out, cell_out, hid32)


def call(kernel, outs, scratch, *args, far=0, us=1):
    return pl.pallas_call(
        kernel,
        out_shape=[jax.ShapeDtypeStruct(s, d) for s, d in outs],
        in_specs=[pl.BlockSpec(memory_space=pltpu.HBM)] * far
        + [pl.BlockSpec(memory_space=pltpu.VMEM)] * (len(args) - far),
        out_specs=[pl.BlockSpec(memory_space=pltpu.VMEM)] * len(outs),
        scratch_shapes=[pltpu.VMEM(s, d) for s, d in scratch] + ([pltpu.SemaphoreType.DMA((far,))] if far else []),
        cost_estimate=pl.CostEstimate(flops=int(us * 1e9), bytes_accessed=0, transcendentals=0),
        compiler_params=pltpu.CompilerParams(vmem_limit_bytes=24 << 20),
    )(*[pltpu.with_memory_space_constraint(a, pltpu.HBM) if i < far else a for i, a in enumerate(args)])


def shards(inputs, hidden_init, cell_init, w_input, w_hidden, gate_bias):
    ch, rows, cols = hidden_init.shape
    gate = 4 * ch
    depth = w_hidden.shape[3]
    cin = w_input.shape[3]
    hid = hidden_init.reshape(ch * rows, cols)
    cell = cell_init.reshape(ch * rows, cols)
    inp = inputs.reshape(-1, cols)
    wx = jnp.transpose(w_input, (0, 1, 3, 2)).reshape(25 * cin, gate)
    bias = gate_bias.reshape(1, gate)
    to_left, to_right, main = call(
        pack_kernel,
        [((FOLD + 8, 128), F32), ((FOLD + 8, 128), F32), ((4 * ch, 128), BF16)],
        [(hid.shape, BF16), (cell.shape, F32), (inp.shape, BF16), (hid.shape, F32), (inp.shape, F32)],
        hid, cell, inp, far=3, us=1,
    )
    n = lax.axis_size("lon")
    from_right = lax.ppermute(to_left, "lon", [((i + 1) % n, i) for i in range(n)])
    from_left = lax.ppermute(to_right, "lon", [(i, (i + 1) % n) for i in range(n)])
    (field,) = call(join_kernel, [((4 * ch + FOLD, 128), BF16)], [], main, from_left, from_right)
    shards = lax.axis_size("chan")
    for step in range(STEPS):
        last = step == STEPS - 1
        wide = 512 if last else 640
        stack = [((25 * cin + 16, wide), BF16), ((25 * cin + 16, gate), BF16)]
        inp32 = (inp.shape, F32)
        hid32 = ((4 * ch, 128), F32)
        pre = ((wide // 128, gate, 128), F32)
        outs = [((4 * ch + (0 if last else FOLD), 128), BF16), ((4 * ch, 128), F32)]
        if shards == 4 and 2 * ch == 128:
            other, same, cross = [
                lax.ppermute(field, "chan", [(i, i ^ k) for i in range(shards)]) for k in (1, 2, 3)
            ]
            windowed = ((5, 2 * ch, 768), BF16)
            (part,) = call(
                functools.partial(near_kernel, step), [pre], [windowed, *stack, inp32],
                field, other, from_left, from_right, inp, w_hidden, wx, bias, us=1.5,
            )
            field, cell = call(
                functools.partial(far_kernel, step), outs, [windowed, pre, hid32],
                same, cross, part, from_left, from_right, cell, w_hidden, us=2,
            )
        else:
            gathered = lax.all_gather(field, "chan", axis=0)
            field, cell = call(
                functools.partial(whole_kernel, step), outs,
                [((5, depth, 768), BF16), *stack, pre, inp32, hid32],
                gathered, from_left, from_right, inp, cell, w_hidden, wx, bias, us=3,
            )
    return field.reshape(ch, rows, cols), cell.reshape(ch, rows, cols)


def solution(mesh):
    in_specs = (
        P(None, None, "groups", "lon"),
        P("chan", "groups", "lon"),
        P("chan", "groups", "lon"),
        P(None, None, "chan", None),
        P(None, None, "chan", None),
        P("chan"),
    )
    out_specs = (P("chan", "groups", "lon"), P("chan", "groups", "lon"))
    return jax.shard_map(shards, mesh=mesh, in_specs=in_specs, out_specs=out_specs, check_vma=False)
```

```python
import functools

import jax
import jax.numpy as jnp
from jax import lax
from jax.experimental import pallas as pl
from jax.experimental.pallas import tpu as pltpu
from jax.sharding import PartitionSpec as P

STEPS = 2
FOLD = 16
F32, BF16 = jnp.float32, jnp.bfloat16


def lanes(rows):
    return lax.broadcasted_iota(jnp.int32, (rows, 128), 1)


def roll(x, by):
    by = by % 128
    return pltpu.roll(x, by, 1) if by else x


def unfold(block, channels):
    return jnp.concatenate(
        [roll(block[8 * (i // 4) : 8 * (i // 4) + 8], -32 * (i % 4)) for i in range(channels // 8)], axis=0
    )


def fold(field):
    lane = lanes(8)
    parts = [jnp.zeros((8, 128), F32) for _ in range(FOLD // 8)]
    for i in range(field.shape[0] // 8):
        base = 32 * (i % 4)
        here = (lane >= base) & (lane < base + 32)
        parts[i // 4] = jnp.where(here, roll(field[8 * i : 8 * i + 8], base), parts[i // 4])
    return jnp.concatenate(parts, axis=0)


def edges_of(rows, groups, vectors):
    lane = lanes(8)
    left = [jnp.zeros((8, 128), F32) for _ in range(vectors)]
    right = [jnp.zeros((8, 128), F32) for _ in range(vectors)]
    for i in range(groups):
        for y in range(4):
            base = 32 * (i % 4) + 8 * y
            moved = roll(rows(i, y), base + 4)
            left[i // 4] = jnp.where((lane >= base + 4) & (lane < base + 8), moved, left[i // 4])
            right[i // 4] = jnp.where((lane >= base) & (lane < base + 4), moved, right[i // 4])
    return jnp.concatenate(left, axis=0), jnp.concatenate(right, axis=0)


def pack_kernel(hid_far, cell_far, inp_far, to_right, to_left, hid_out, hid, cell, inp, hid32, inp32, arrived):
    ch = hid.shape[0] // 4
    pairs = ((hid_far, hid), (cell_far, cell), (inp_far, inp))
    copies = [pltpu.make_async_copy(a, b, arrived.at[i]) for i, (a, b) in enumerate(pairs)]
    for copy in copies:
        copy.start()
    for copy in copies:
        copy.wait()
    hid32[...] = hid[...].astype(F32)
    inp32[...] = inp[...].astype(F32)
    hl, hr = edges_of(lambda i, y: hid32[pl.ds(32 * i + y, 8, stride=4), :], ch // 8, 2)
    cl, cr = edges_of(lambda i, y: cell[pl.ds(32 * i + y, 8, stride=4), :], ch // 8, 2)
    il, ir = edges_of(lambda i, y: inp32[pl.ds(32 * i + y, 8, stride=4), :], inp.shape[0] // 32, 1)
    to_left[0:FOLD] = hl + roll(cl, -4)
    to_left[FOLD:] = il
    to_right[0:FOLD] = hr + roll(cr, 4)
    to_right[FOLD:] = ir
    hid_out[...] = hid32[...]


def main_kernel(hid, main):
    ch = hid.shape[0] // 4
    for y in range(4):
        main[y * ch : (y + 1) * ch, :] = hid[pl.ds(y, ch, stride=4), :].astype(BF16)


def strip_kernel(came_left, came_right, to_right, to_left, from_right, from_left, out):
    from_left[...], from_right[...] = came_left[...], came_right[...]
    low = (lanes(FOLD) & 7) < 4
    out[0:FOLD] = jnp.where(low, from_left[0:FOLD], from_right[0:FOLD]).astype(BF16)
    out[FOLD:] = jnp.where(low, to_right[0:FOLD], to_left[0:FOLD]).astype(BF16)


def windows(row, halo, y):
    if halo is None:
        return [roll(row, -d) for d in range(-2, 3)]
    lane = lanes(row.shape[0])
    ring = roll(halo, -(8 * y + 4))
    out = []
    for d in range(-2, 3):
        if d == 0:
            out.append(row)
        else:
            other = lane >= 128 + d if d < 0 else lane < d
            out.append(roll(jnp.where(other, ring, row), -d))
    return out


def strips(halo, own):
    lane = lanes(halo.shape[0])
    low, left, used = (lane & 7) < 4, lane < 64, lane < 32
    halo, own = [jnp.where(used, x, jnp.zeros_like(x)) for x in (halo, own)]
    return jnp.where(
        left, jnp.where(low, roll(halo, 16), roll(own, 16)), jnp.where(low, roll(own, 80), roll(halo, 80))
    )


def own_edges(rows):
    lane = lanes(rows[0].shape[0])
    own = jnp.zeros_like(rows[0])
    for y in range(4):
        own = jnp.where((lane >= 8 * y) & (lane < 8 * y + 8), roll(rows[y], 8 * y + 4), own)
    return own


def sigmoid(x):
    return 0.5 * jnp.tanh(0.5 * x) + 0.5


def gates(pre, ch, at, cell):
    part = [pre[at, pl.ds(g, ch, stride=4), :] for g in range(4)]
    cell = sigmoid(part[1]) * cell + sigmoid(part[0]) * jnp.tanh(part[2])
    return sigmoid(part[3]) * jnp.tanh(cell), cell


DRIVE = (((0,), (0,)), ((), ()))


def near_far(own, other, ch):
    even = lax.axis_index("chan") % 2 == 0
    low, high = jnp.where(even, own, other), jnp.where(even, other, own)
    return rows_of([low, high], ch)


def rows_of(shards, ch):
    rows = [jnp.concatenate([s[y * ch : (y + 1) * ch] for s in shards], axis=0) for y in range(4)]
    if shards[0].shape[0] == 4 * ch:
        return rows, None
    halo = jnp.concatenate([unfold(s[4 * ch : 4 * ch + FOLD].astype(F32), ch) for s in shards], axis=0)
    return rows, halo.astype(BF16)


def store_windows(xs, rows, halo):
    depth = rows[0].shape[0]
    for b in range(5):
        xs[b, :, 0:128] = jnp.zeros((depth, 128), BF16)
        xs[b, :, 640:768] = jnp.zeros((depth, 128), BF16)
    for y in range(4):
        for b, window in enumerate(windows(rows[y], halo, y)):
            xs[b, :, 128 * (y + 1) : 128 * (y + 2)] = window


def hidden_rows(w, xs, at, pair):
    depth = xs.shape[1]
    terms = [(a, b, 2 * pair + a - 2) for a in range(5) for b in range(5) if -2 < 2 * pair + a - 2 < 4]
    left = jnp.concatenate([w[a, b, :, pl.ds(at, depth)] for a, b, _ in terms], axis=1)
    right = jnp.concatenate([xs[b, :, 128 * (lo + 1) : 128 * (lo + 3)] for _, b, lo in terms], axis=0)
    return jnp.dot(left, right, preferred_element_type=F32)


def hidden_rim(w, strip):
    stack = jnp.concatenate([roll(strip, -8 * (a - 2)) for a in range(5)], axis=0)
    total = None
    for b in range(5):
        left = jnp.concatenate([w[a, b] for a in range(5)], axis=1)
        part = roll(jnp.dot(left, stack, preferred_element_type=F32), -(b - 2))
        total = part if total is None else total + part
    return total


def input_rows(step, inp32, inp, from_right, from_left):
    cin = inp.shape[0] // (4 * STEPS)
    inp32[...] = inp[...].astype(F32)
    rows = [inp32[pl.ds(4 * cin * step + y, cin, stride=4), :].astype(BF16) for y in range(4)]
    low = (lanes(8) & 7) < 4
    block = jnp.where(low, from_left[FOLD:], from_right[FOLD:])
    first = step * cin // 8
    halo = jnp.concatenate([roll(block, -32 * i) for i in range(first, first + cin // 8)], axis=0).astype(BF16)
    return rows, halo


def store_inputs(xi, rows, halo):
    cin = halo.shape[0]
    wins = [windows(rows[y], halo, y) for y in range(4)]
    for a in range(5):
        for b in range(5):
            at = cin * (5 * a + b)
            for y in range(4):
                r = y + a - 2
                xi[at : at + cin, 128 * y : 128 * (y + 1)] = (
                    wins[r][b] if 0 <= r < 4 else jnp.zeros((cin, 128), BF16)
                )
    store_ones(xi, 25 * cin)


def store_input_rim(xi, rows, halo):
    cin = halo.shape[0]
    strip = strips(halo, own_edges(rows))
    for a in range(5):
        for b in range(5):
            at = cin * (5 * a + b)
            xi[at : at + cin, :] = roll(strip, -(8 * (a - 2) + b - 2))
    store_ones(xi, 25 * cin)


def store_ones(xi, taps):
    ones = lax.broadcasted_iota(jnp.int32, (16, xi.shape[1]), 0) < 3
    xi[taps : taps + 16, :] = jnp.where(ones, 1.0, 0.0).astype(BF16)


def store_input_weights(wxb, wx, bias):
    taps = wx.shape[0]
    wxb[0:taps, :] = wx[...]
    b0 = bias[...]
    b1 = b0.astype(BF16).astype(F32)
    b2 = (b0 - b1).astype(BF16).astype(F32)
    b3 = b0 - b1 - b2
    sub = lax.broadcasted_iota(jnp.int32, (16, wxb.shape[1]), 0)
    wxb[taps : taps + 16, :] = jnp.where(
        sub == 0, b1, jnp.where(sub == 1, b2, jnp.where(sub == 2, b3, 0.0))
    ).astype(BF16)


def input_part(wxb, xi, at, wide):
    return lax.dot_general(wxb[...], xi[:, at : at + wide], DRIVE, preferred_element_type=F32)


def rim_gates(pre, to_right, to_left, from_right, from_left, ch):
    low = (lanes(FOLD) & 7) < 4
    halo = unfold(jnp.where(low, from_right[0:FOLD], from_left[0:FOLD]), ch)
    own = unfold(jnp.where(low, to_left[0:FOLD], to_right[0:FOLD]), ch)
    halo, own = [jnp.where((lanes(ch) & 7) < 4, roll(x, -4), roll(x, 4)) for x in (halo, own)]
    return gates(pre, ch, 0, strips(halo, own))


def rim_fold(h):
    h = jnp.where((lanes(h.shape[0]) & 7) < 4, roll(h, -16), roll(h, -80))
    return fold(h).astype(BF16)


def patch(row, rim, y):
    lane = lanes(row.shape[0])
    base = 8 * y + 16
    row = jnp.where(lane < 2, roll(rim, -(base + 4)), row)
    return jnp.where(lane >= 126, roll(rim, 60 - base), row)


def finish(step, pre, cell, hid_out, cell_out, hid32):
    ch = cell.shape[0] // 4
    last = step == STEPS - 1
    for y in range(4):
        before = cell[pl.ds(y, ch, stride=4), :] if step == 0 else cell[y * ch : (y + 1) * ch, :]
        h, c = gates(pre, ch, y, before)
        if last:
            cell_out[pl.ds(y, ch, stride=4), :] = c
            hid32[pl.ds(y, ch, stride=4), :] = h
        else:
            cell_out[y * ch : (y + 1) * ch, :] = c
            hid_out[y * ch : (y + 1) * ch, :] = h.astype(BF16)
    if last:
        hid_out[...] = hid32[...].astype(BF16)


def whole_kernel(step, gathered, from_right, from_left, inp, cell, w, wx, bias, hid_out, cell_out, xs, xi, wxb, pre, inp32, hid32):
    shards, ch = gathered.shape[0], cell.shape[0] // 4
    store_windows(xs, *rows_of([gathered[c] for c in range(shards)], ch))
    store_inputs(xi, *input_rows(step, inp32, inp, from_right, from_left))
    store_input_weights(wxb, wx, bias)
    for pair in range(2):
        total = hidden_rows(w, xs, 0, pair) + input_part(wxb, xi, 256 * pair, 256)
        pre[2 * pair] = total[:, 0:128]
        pre[2 * pair + 1] = total[:, 128:256]
    finish(step, pre, cell, hid_out, cell_out, hid32)


def first_channel(depth, remote):
    mine = lax.axis_index("chan") // 2
    return pl.multiple_of((1 - mine if remote else mine) * depth, depth)


def after_kernel(x, before, out):
    out[...] = x[...]


def near_kernel(step, own, other, from_right, from_left, inp, w, wx, bias, part, xs, xi, wxb, inp32):
    ch = w.shape[2] // 4
    at = first_channel(2 * ch, False)
    store_windows(xs, *near_far(own[...], other[...], ch))
    store_inputs(xi, *input_rows(step, inp32, inp, from_right, from_left))
    store_input_weights(wxb, wx, bias)
    for pair in range(2):
        total = hidden_rows(w, xs, at, pair) + input_part(wxb, xi, 256 * pair, 256)
        part[2 * pair] = total[:, 0:128]
        part[2 * pair + 1] = total[:, 128:256]


def far_kernel(step, same, cross, part, cell, w, hid_out, cell_out, xs, pre, hid32):
    ch = cell.shape[0] // 4
    at = first_channel(2 * ch, True)
    store_windows(xs, *near_far(same[...], cross[...], ch))
    for pair in range(2):
        total = hidden_rows(w, xs, at, pair)
        pre[2 * pair] = part[2 * pair] + total[:, 0:128]
        pre[2 * pair + 1] = part[2 * pair + 1] + total[:, 128:256]
    finish(step, pre, cell, hid_out, cell_out, hid32)


def rim_kernel(*refs):
    *blocks, hid, cell, to_right, to_left, from_right, from_left, inp, w, wx, bias = refs[:-6]
    hid_out, cell_out, xi, wxb, pre, inp32 = refs[-6:]
    ch = cell.shape[0] // 4
    if len(blocks) == 4:
        even, first = lax.axis_index("chan") % 2 == 0, lax.axis_index("chan") // 2 == 0
        own, other, same, cross = [b[...] for b in blocks]
        here = (jnp.where(even, own, other), jnp.where(even, other, own))
        there = (jnp.where(even, same, cross), jnp.where(even, cross, same))
        shards = [jnp.where(first, here[k], there[k]) for k in (0, 1)]
        shards += [jnp.where(first, there[k], here[k]) for k in (0, 1)]
    else:
        shards = [blocks[0][c] for c in range(blocks[0].shape[0])]
    halo = jnp.concatenate([unfold(s[0:FOLD].astype(F32), ch) for s in shards], axis=0).astype(BF16)
    own = jnp.concatenate([unfold(s[FOLD:].astype(F32), ch) for s in shards], axis=0).astype(BF16)
    store_input_rim(xi, *input_rows(0, inp32, inp, from_right, from_left))
    store_input_weights(wxb, wx, bias)
    pre[0] = hidden_rim(w, strips(halo, own)) + input_part(wxb, xi, 0, 128)
    h, c = rim_gates(pre, to_right, to_left, from_right, from_left, ch)
    for y in range(4):
        at = slice(y * ch, (y + 1) * ch)
        hid_out[at, :] = patch(hid[at, :].astype(F32), h, y).astype(BF16)
        cell_out[at, :] = patch(cell[at, :], c, y)
    hid_out[4 * ch : 4 * ch + FOLD, :] = rim_fold(h)


def call(kernel, outs, scratch, *args, far=0, us=1):
    return pl.pallas_call(
        kernel,
        out_shape=[jax.ShapeDtypeStruct(s, d) for s, d in outs],
        in_specs=[pl.BlockSpec(memory_space=pltpu.HBM)] * far
        + [pl.BlockSpec(memory_space=pltpu.VMEM)] * (len(args) - far),
        out_specs=[pl.BlockSpec(memory_space=pltpu.VMEM)] * len(outs),
        scratch_shapes=[pltpu.VMEM(s, d) for s, d in scratch] + ([pltpu.SemaphoreType.DMA((far,))] if far else []),
        cost_estimate=pl.CostEstimate(flops=int(us * 1e9), bytes_accessed=0, transcendentals=0),
        compiler_params=pltpu.CompilerParams(vmem_limit_bytes=24 << 20),
    )(*[pltpu.with_memory_space_constraint(a, pltpu.HBM) if i < far else a for i, a in enumerate(args)])


def shards(inputs, hidden_init, cell_init, w_input, w_hidden, gate_bias):
    ch, rows, cols = hidden_init.shape
    gate = 4 * ch
    depth = w_hidden.shape[3]
    cin = w_input.shape[3]
    hid = hidden_init.reshape(ch * rows, cols)
    cell = cell_init.reshape(ch * rows, cols)
    inp = inputs.reshape(-1, cols)
    wx = jnp.transpose(w_input, (0, 1, 3, 2)).reshape(25 * cin, gate)
    bias = gate_bias.reshape(1, gate)
    to_right, to_left, hid = call(
        pack_kernel,
        [((FOLD + 8, 128), F32), ((FOLD + 8, 128), F32), ((4 * ch, 128), F32)],
        [(hid.shape, BF16), (cell.shape, F32), (inp.shape, BF16), (hid.shape, F32), (inp.shape, F32)],
        hid, cell, inp, far=3, us=1,
    )
    (main,) = call(main_kernel, [((4 * ch, 128), BF16)], [], hid, us=0.01)
    n = lax.axis_size("lon")
    came_left = lax.ppermute(to_right, "lon", [(i, (i + 1) % n) for i in range(n)])
    came_right = lax.ppermute(to_left, "lon", [((i + 1) % n, i) for i in range(n)])
    from_right, from_left, strip = call(
        strip_kernel, [(to_left.shape, F32), (to_left.shape, F32), ((2 * FOLD, 128), BF16)], [],
        came_left, came_right, to_right, to_left,
    )
    shards = lax.axis_size("chan")
    paired = shards == 4 and 2 * ch == 128

    def others(x):
        return [lax.ppermute(x, "chan", [(i, i ^ k) for i in range(shards)]) for k in (1, 2)]

    def onward(same, before):
        (same,) = call(after_kernel, [(same.shape, BF16)], [], same, before, us=0.01)
        return same, lax.ppermute(same, "chan", [(i, i ^ 1) for i in range(shards)])

    field = main
    traveling = [lax.ppermute(field, "chan", [(i, i ^ k) for i in range(shards)]) for k in (1, 2, 3)] if paired else None
    blocks = [strip, *[lax.ppermute(strip, "chan", [(i, i ^ k) for i in range(shards)]) for k in (1, 2, 3)]] if paired else [lax.all_gather(strip, "chan", axis=0)]
    kinds = [((25 * cin + 16, gate), BF16)]
    for step in range(STEPS):
        last = step == STEPS - 1
        stack = [((25 * cin + 16, 512), BF16), *kinds]
        inp32 = (inp.shape, F32)
        hid32 = ((4 * ch, 128), F32)
        pre = ((4, gate, 128), F32)
        outs = [((4 * ch, 128), BF16), ((4 * ch, 128), F32)]
        if paired:
            other, same, *cross = traveling
            windowed = ((5, 2 * ch, 768), BF16)
            (part,) = call(
                functools.partial(near_kernel, step), [pre], [windowed, *stack, inp32],
                field, other, from_right, from_left, inp, w_hidden, wx, bias, us=0.01,
            )
            if cross:
                (cross,) = cross
            else:
                same, cross = onward(same, part)
            field, cell = call(
                functools.partial(far_kernel, step), outs, [windowed, pre, hid32],
                same, cross, part, cell, w_hidden, us=0.01,
            )
        else:
            gathered = lax.all_gather(field, "chan", axis=0)
            field, cell = call(
                functools.partial(whole_kernel, step), outs,
                [((5, depth, 768), BF16), *stack, pre, inp32, hid32],
                gathered, from_right, from_left, inp, cell, w_hidden, wx, bias, us=3,
            )
        if not last:
            field, cell = call(
                rim_kernel, [((4 * ch + FOLD, 128), BF16), ((4 * ch, 128), F32)],
                [((25 * cin + 16, 128), BF16), *kinds, ((1, gate, 128), F32), inp32],
                *blocks, field, cell, to_right, to_left, from_right, from_left, inp, w_hidden, wx, bias, us=0.01,
            )
            traveling = others(field) if paired else None
    return field.reshape(ch, rows, cols), cell.reshape(ch, rows, cols)


def solution(mesh):
    in_specs = (
        P(None, None, "groups", "lon"),
        P("chan", "groups", "lon"),
        P("chan", "groups", "lon"),
        P(None, None, "chan", None),
        P(None, None, "chan", None),
        P("chan"),
    )
    out_specs = (P("chan", "groups", "lon"), P("chan", "groups", "lon"))
    return jax.shard_map(shards, mesh=mesh, in_specs=in_specs, out_specs=out_specs, check_vma=False)
```

```python
import functools

import jax
import jax.numpy as jnp
from jax import lax
from jax.experimental import pallas as pl
from jax.experimental.pallas import tpu as pltpu
from jax.sharding import PartitionSpec as P

STEPS = 2
FOLD = 16
F32, BF16 = jnp.float32, jnp.bfloat16


def lanes(rows):
    return lax.broadcasted_iota(jnp.int32, (rows, 128), 1)


def roll(x, by):
    by = by % 128
    return pltpu.roll(x, by, 1) if by else x


def unfold(block, channels):
    return jnp.concatenate(
        [roll(block[8 * (i // 4) : 8 * (i // 4) + 8], -32 * (i % 4)) for i in range(channels // 8)], axis=0
    )


def fold(field):
    lane = lanes(8)
    parts = [jnp.zeros((8, 128), F32) for _ in range(FOLD // 8)]
    for i in range(field.shape[0] // 8):
        base = 32 * (i % 4)
        here = (lane >= base) & (lane < base + 32)
        parts[i // 4] = jnp.where(here, roll(field[8 * i : 8 * i + 8], base), parts[i // 4])
    return jnp.concatenate(parts, axis=0)


def edges_of(rows, groups, vectors):
    lane = lanes(8)
    left = [jnp.zeros((8, 128), F32) for _ in range(vectors)]
    right = [jnp.zeros((8, 128), F32) for _ in range(vectors)]
    for i in range(groups):
        for y in range(4):
            base = 32 * (i % 4) + 8 * y
            moved = roll(rows(i, y), base + 4)
            left[i // 4] = jnp.where((lane >= base + 4) & (lane < base + 8), moved, left[i // 4])
            right[i // 4] = jnp.where((lane >= base) & (lane < base + 4), moved, right[i // 4])
    return jnp.concatenate(left, axis=0), jnp.concatenate(right, axis=0)


def pack_kernel(*refs):
    fars, (to_right, to_left, hid_out, weights, part) = refs[:5], refs[5:10]
    hid, cell, inp, wx, bias, hid32, inp32, xi, arrived = refs[10:]
    ch = hid.shape[0] // 4
    pairs = tuple(zip(fars, (hid, cell, inp, wx, bias)))
    copies = [pltpu.make_async_copy(a, b, arrived.at[i]) for i, (a, b) in enumerate(pairs)]
    for copy in copies:
        copy.start()
    for copy in copies:
        copy.wait()
    hid32[...] = hid[...].astype(F32)
    inp32[...] = inp[...].astype(F32)
    hl, hr = edges_of(lambda i, y: hid32[pl.ds(32 * i + y, 8, stride=4), :], ch // 8, 2)
    cl, cr = edges_of(lambda i, y: cell[pl.ds(32 * i + y, 8, stride=4), :], ch // 8, 2)
    il, ir = edges_of(lambda i, y: inp32[pl.ds(32 * i + y, 8, stride=4), :], inp.shape[0] // 32, 1)
    to_left[0:FOLD] = hl + roll(cl, -4)
    to_left[FOLD:] = il
    to_right[0:FOLD] = hr + roll(cr, 4)
    to_right[FOLD:] = ir
    hid_out[...] = hid32[...]

    @pl.when(lax.axis_index("lon") == 0)
    def _():
        drive(inp, inp32, wx, bias, weights, part, xi)


def main_kernel(hid, main):
    ch = hid.shape[0] // 4
    for y in range(4):
        main[y * ch : (y + 1) * ch, :] = hid[pl.ds(y, ch, stride=4), :].astype(BF16)


def strip_kernel(came_left, came_right, to_right, to_left, from_right, from_left, out):
    from_left[...], from_right[...] = came_left[...], came_right[...]
    low = (lanes(FOLD) & 7) < 4
    out[0:FOLD] = jnp.where(low, from_left[0:FOLD], from_right[0:FOLD]).astype(BF16)
    out[FOLD:] = jnp.where(low, to_right[0:FOLD], to_left[0:FOLD]).astype(BF16)


def windows(row, halo, y):
    if halo is None:
        return [roll(row, -d) for d in range(-2, 3)]
    lane = lanes(row.shape[0])
    ring = roll(halo, -(8 * y + 4))
    out = []
    for d in range(-2, 3):
        if d == 0:
            out.append(row)
        else:
            other = lane >= 128 + d if d < 0 else lane < d
            out.append(roll(jnp.where(other, ring, row), -d))
    return out


def strips(halo, own):
    lane = lanes(halo.shape[0])
    low, left, used = (lane & 7) < 4, lane < 64, lane < 32
    halo, own = [jnp.where(used, x, jnp.zeros_like(x)) for x in (halo, own)]
    return jnp.where(
        left, jnp.where(low, roll(halo, 16), roll(own, 16)), jnp.where(low, roll(own, 80), roll(halo, 80))
    )


def own_edges(rows):
    lane = lanes(rows[0].shape[0])
    own = jnp.zeros_like(rows[0])
    for y in range(4):
        own = jnp.where((lane >= 8 * y) & (lane < 8 * y + 8), roll(rows[y], 8 * y + 4), own)
    return own


def sigmoid(x):
    return 0.5 * jnp.tanh(0.5 * x) + 0.5


def gates(pre, ch, at, cell):
    part = [pre[at, pl.ds(g, ch, stride=4), :] for g in range(4)]
    cell = sigmoid(part[1]) * cell + sigmoid(part[0]) * jnp.tanh(part[2])
    return sigmoid(part[3]) * jnp.tanh(cell), cell


def near_far(own, other, ch):
    return rows_of(ordered(own, other), ch)


def rows_of(shards, ch):
    rows = [jnp.concatenate([s[y * ch : (y + 1) * ch] for s in shards], axis=0) for y in range(4)]
    if shards[0].shape[0] == 4 * ch:
        return rows, None
    halo = jnp.concatenate([unfold(s[4 * ch : 4 * ch + FOLD].astype(F32), ch) for s in shards], axis=0)
    return rows, halo.astype(BF16)


def store_windows(xs, rows, halo):
    depth = rows[0].shape[0]
    for b in range(5):
        xs[b, :, 0:128] = jnp.zeros((depth, 128), BF16)
        xs[b, :, 640:768] = jnp.zeros((depth, 128), BF16)
    for y in range(4):
        for b, window in enumerate(windows(rows[y], halo, y)):
            xs[b, :, 128 * (y + 1) : 128 * (y + 2)] = window


def hidden_rows(w, xs, at, pair):
    depth = xs.shape[1]
    terms = [(a, b, 2 * pair + a - 2) for a in range(5) for b in range(5) if -2 < 2 * pair + a - 2 < 4]
    left = jnp.concatenate([w[a, b, :, pl.ds(at, depth)] for a, b, _ in terms], axis=1)
    right = jnp.concatenate([xs[b, :, 128 * (lo + 1) : 128 * (lo + 3)] for _, b, lo in terms], axis=0)
    return jnp.dot(left, right, preferred_element_type=F32)


def hidden_rim(w, strip, at):
    stack = jnp.concatenate([roll(strip, -8 * (a - 2)) for a in range(5)], axis=0)
    total = None
    for b in range(5):
        left = jnp.concatenate([w[a, b, :, pl.ds(at, strip.shape[0])] for a in range(5)], axis=1)
        part = roll(jnp.dot(left, stack, preferred_element_type=F32), -(b - 2))
        total = part if total is None else total + part
    return total


def input_rows(step, inp32, inp, from_right, from_left):
    cin = inp.shape[0] // (4 * STEPS)
    inp32[...] = inp[...].astype(F32)
    rows = [inp32[pl.ds(4 * cin * step + y, cin, stride=4), :].astype(BF16) for y in range(4)]
    low = (lanes(8) & 7) < 4
    block = jnp.where(low, from_left[FOLD:], from_right[FOLD:])
    first = step * cin // 8
    halo = jnp.concatenate([roll(block, -32 * i) for i in range(first, first + cin // 8)], axis=0).astype(BF16)
    return rows, halo


def store_inputs(xi, rows, halo):
    cin = rows[0].shape[0]
    wins = [windows(rows[y], halo, y) for y in range(4)]
    for a in range(5):
        for b in range(5):
            at = cin * (5 * a + b)
            for y in range(4):
                r = y + a - 2
                xi[at : at + cin, 128 * y : 128 * (y + 1)] = (
                    wins[r][b] if 0 <= r < 4 else jnp.zeros((cin, 128), BF16)
                )
    store_ones(xi, 25 * cin)


def store_input_rim(xi, rows, halo):
    cin = halo.shape[0]
    strip = strips(halo, own_edges(rows))
    for a in range(5):
        for b in range(5):
            at = cin * (5 * a + b)
            xi[at : at + cin, :] = roll(strip, -(8 * (a - 2) + b - 2))
    store_ones(xi, 25 * cin)


def store_ones(xi, taps):
    ones = lax.broadcasted_iota(jnp.int32, (16, xi.shape[1]), 0) < 3
    xi[taps : taps + 16, :] = jnp.where(ones, 1.0, 0.0).astype(BF16)
    xi[taps + 16 :, :] = jnp.zeros((xi.shape[0] - taps - 16, xi.shape[1]), BF16)


def input_weights(wx, bias):
    taps, gate = wx.shape
    b0 = bias[...]
    b1 = b0.astype(BF16).astype(F32)
    b2 = (b0 - b1).astype(BF16).astype(F32)
    b3 = b0 - b1 - b2
    sub = lax.broadcasted_iota(jnp.int32, (16, gate), 0)
    extra = jnp.where(sub == 0, b1, jnp.where(sub == 1, b2, jnp.where(sub == 2, b3, 0.0)))
    blank = jnp.zeros((padded(taps) - taps - 16, gate), F32)
    return jnp.concatenate([wx[...].astype(F32), extra, blank], axis=0).T.astype(BF16)


def padded(taps):
    return (taps + 16 + 127) // 128 * 128


def drive(inp, inp32, wx, bias, weights, part, xi):
    cin = inp.shape[0] // (4 * STEPS)
    inp32[...] = inp[...].astype(F32)
    weights[...] = input_weights(wx, bias)
    store_inputs(xi, [inp32[pl.ds(y, cin, stride=4), :].astype(BF16) for y in range(4)], None)
    for pair in range(2):
        total = input_part(weights, xi, 256 * pair, 256)
        part[2 * pair] = total[:, 0:128]
        part[2 * pair + 1] = total[:, 128:256]


def drive_kernel(inp, wx, bias, weights_in, part_in, weights, part, inp32, xi):
    @pl.when(lax.axis_index("lon") != 0)
    def _():
        drive(inp, inp32, wx, bias, weights, part, xi)


def input_part(weights, xi, at, wide):
    return jnp.dot(weights[...], xi[:, at : at + wide], preferred_element_type=F32)


def rim_gates(pre, to_right, to_left, from_right, from_left, ch):
    low = (lanes(FOLD) & 7) < 4
    halo = unfold(jnp.where(low, from_right[0:FOLD], from_left[0:FOLD]), ch)
    own = unfold(jnp.where(low, to_left[0:FOLD], to_right[0:FOLD]), ch)
    halo, own = [jnp.where((lanes(ch) & 7) < 4, roll(x, -4), roll(x, 4)) for x in (halo, own)]
    return gates(pre, ch, 0, strips(halo, own))


def rim_fold(h):
    h = jnp.where((lanes(h.shape[0]) & 7) < 4, roll(h, -16), roll(h, -80))
    return fold(h).astype(BF16)


def patch(row, rim, y):
    lane = lanes(row.shape[0])
    base = 8 * y + 16
    row = jnp.where(lane < 2, roll(rim, -(base + 4)), row)
    return jnp.where(lane >= 126, roll(rim, 60 - base), row)


def finish(step, pre, cell, hid_out, cell_out, hid32):
    ch = cell.shape[0] // 4
    last = step == STEPS - 1
    for y in range(4):
        before = cell[pl.ds(y, ch, stride=4), :] if step == 0 else cell[y * ch : (y + 1) * ch, :]
        h, c = gates(pre, ch, y, before)
        if last:
            cell_out[pl.ds(y, ch, stride=4), :] = c
            hid32[pl.ds(y, ch, stride=4), :] = h
        else:
            cell_out[y * ch : (y + 1) * ch, :] = c
            hid_out[y * ch : (y + 1) * ch, :] = h.astype(BF16)
    if last:
        hid_out[...] = hid32[...].astype(BF16)


def whole_kernel(step, gathered, driven, cell, w, hid_out, cell_out, xs, pre, hid32):
    shards, ch = gathered.shape[0], cell.shape[0] // 4
    store_windows(xs, *rows_of([gathered[c] for c in range(shards)], ch))
    for pair in range(2):
        total = hidden_rows(w, xs, 0, pair)
        pre[2 * pair] = driven[2 * pair] + total[:, 0:128]
        pre[2 * pair + 1] = driven[2 * pair + 1] + total[:, 128:256]
    finish(step, pre, cell, hid_out, cell_out, hid32)


def first_channel(depth, remote):
    mine = lax.axis_index("chan") // 2
    return pl.multiple_of((1 - mine if remote else mine) * depth, depth)


def after_kernel(x, before, out):
    out[...] = x[...]


def near_kernel(own, other, driven, w, part, xs):
    ch = w.shape[2] // 4
    at = first_channel(2 * ch, False)
    store_windows(xs, *near_far(own, other, ch))
    for pair in range(2):
        total = hidden_rows(w, xs, at, pair)
        part[2 * pair] = driven[2 * pair] + total[:, 0:128]
        part[2 * pair + 1] = driven[2 * pair + 1] + total[:, 128:256]


def next_drive_kernel(step, from_right, from_left, inp, weights, before, part, xi, inp32):
    store_inputs(xi, *input_rows(step, inp32, inp, from_right, from_left))
    for pair in range(2):
        total = input_part(weights, xi, 256 * pair, 256)
        part[2 * pair] = total[:, 0:128]
        part[2 * pair + 1] = total[:, 128:256]


def far_kernel(step, same, cross, part, cell, w, *refs):
    ch = cell.shape[0] // 4
    hid_out, cell_out, xs, pre, hid32 = refs[-5:]
    at = first_channel(2 * ch, True)
    store_windows(xs, *near_far(same, cross, ch))
    for pair in range(2):
        total = hidden_rows(w, xs, at, pair)
        pre[2 * pair] = part[2 * pair] + total[:, 0:128]
        pre[2 * pair + 1] = part[2 * pair + 1] + total[:, 128:256]
    finish(step, pre, cell, hid_out, cell_out, hid32)


SETS = ((1, 2), (3, 4), (0, 3))


def split_kernel(w, before, out):
    half = w.shape[3] // 4
    at = first_channel(2 * half, True)
    even = lax.axis_index("chan") % 2 == 0
    left = lanes(w.shape[2]) < half
    for k, (one, two) in enumerate(SETS):
        for b in range(5):
            x, y = w[one, b, :, pl.ds(at, 2 * half)], w[two, b, :, pl.ds(at, 2 * half)]
            low, high = jnp.where(left, x, roll(y, half)), jnp.where(left, roll(x, half), y)
            out[0, 5 * k + b] = jnp.where(even, low, high)
            out[1, 5 * k + b] = jnp.where(even, high, low)


def shard_rows(weights, which, xs, pair):
    left, right = [], []
    for k in (0, pair + 1):
        for b in range(5):
            left.append(weights[which, 5 * k + b])
            for a in SETS[k]:
                lo = 2 * pair + a - 2
                right.append(xs[b, :, 128 * (lo + 1) : 128 * (lo + 3)])
    return jnp.dot(jnp.concatenate(left, axis=1), jnp.concatenate(right, axis=0), preferred_element_type=F32)


def shard_kernel(step, which, shard, part, weights, *refs):
    *ends, xs = refs if which == 0 else (*refs[:-3], refs[-3])
    ch = shard.shape[0] // 4 - FOLD // 4
    store_windows(xs, *rows_of([shard[...]], ch))
    pre = ends[0] if which == 0 else refs[-2]
    for pair in range(2):
        total = shard_rows(weights, which, xs, pair)
        pre[2 * pair] = part[2 * pair] + total[:, 0:128]
        pre[2 * pair + 1] = part[2 * pair + 1] + total[:, 128:256]
    if which == 1:
        finish(step, pre, *ends, refs[-1])


def rim_strips(shards, ch):
    halo = jnp.concatenate([unfold(s[0:FOLD].astype(F32), ch) for s in shards], axis=0).astype(BF16)
    own = jnp.concatenate([unfold(s[FOLD:].astype(F32), ch) for s in shards], axis=0).astype(BF16)
    return strips(halo, own)


def ordered(own, other):
    even = lax.axis_index("chan") % 2 == 0
    return [jnp.where(even, own[...], other[...]), jnp.where(even, other[...], own[...])]


def rim_drive_kernel(from_right, from_left, inp, weights, *refs):
    part, xi, inp32 = refs[-3:]
    store_input_rim(xi, *input_rows(0, inp32, inp, from_right, from_left))
    part[...] = input_part(weights, xi, 0, 128)


def rim_kernel(*refs):
    *blocks, part, hid, cell, to_right, to_left, from_right, from_left, w, hid_out, cell_out, pre = refs
    ch = cell.shape[0] // 4
    if len(blocks) == 4:
        first = lax.axis_index("chan") // 2 == 0
        here, there = ordered(*blocks[:2]), ordered(*blocks[2:])
        shards = [jnp.where(first, here[k], there[k]) for k in (0, 1)]
        shards += [jnp.where(first, there[k], here[k]) for k in (0, 1)]
    else:
        shards = [blocks[0][c] for c in range(blocks[0].shape[0])]
    pre[0] = part[...] + hidden_rim(w, rim_strips(shards, ch), 0)
    h, c = rim_gates(pre, to_right, to_left, from_right, from_left, ch)
    for y in range(4):
        at = slice(y * ch, (y + 1) * ch)
        hid_out[at, :] = patch(hid[at, :].astype(F32), h, y).astype(BF16)
        cell_out[at, :] = patch(cell[at, :], c, y)
    hid_out[4 * ch : 4 * ch + FOLD, :] = rim_fold(h)


def call(kernel, outs, scratch, *args, far=0, us=1, same=None):
    return pl.pallas_call(
        kernel,
        out_shape=[jax.ShapeDtypeStruct(s, d) for s, d in outs],
        in_specs=[pl.BlockSpec(memory_space=pltpu.HBM)] * far
        + [pl.BlockSpec(memory_space=pltpu.VMEM)] * (len(args) - far),
        out_specs=[pl.BlockSpec(memory_space=pltpu.VMEM)] * len(outs),
        scratch_shapes=[pltpu.VMEM(s, d) for s, d in scratch] + ([pltpu.SemaphoreType.DMA((far,))] if far else []),
        input_output_aliases=same or {},
        cost_estimate=pl.CostEstimate(flops=int(us * 1e9), bytes_accessed=0, transcendentals=0),
        compiler_params=pltpu.CompilerParams(vmem_limit_bytes=24 << 20),
    )(*[pltpu.with_memory_space_constraint(a, pltpu.HBM) if i < far else a for i, a in enumerate(args)])


def shards(inputs, hidden_init, cell_init, w_input, w_hidden, gate_bias):
    ch, rows, cols = hidden_init.shape
    gate = 4 * ch
    depth = w_hidden.shape[3]
    cin = w_input.shape[3]
    hid = hidden_init.reshape(ch * rows, cols)
    cell = cell_init.reshape(ch * rows, cols)
    inp = inputs.reshape(-1, cols)
    wx = jnp.transpose(w_input, (0, 1, 3, 2)).reshape(25 * cin, gate)
    bias = gate_bias.reshape(1, gate)
    driven = [((gate, padded(25 * cin)), BF16), ((4, gate, 128), F32)]
    stack = ((padded(25 * cin), 512), BF16)
    inp32 = (inp.shape, F32)
    to_right, to_left, hid, weights, part = call(
        pack_kernel,
        [((FOLD + 8, 128), F32), ((FOLD + 8, 128), F32), ((4 * ch, 128), F32), *driven],
        [(hid.shape, BF16), (cell.shape, F32), (inp.shape, BF16), (wx.shape, BF16), (bias.shape, F32),
         (hid.shape, F32), inp32, stack],
        hid, cell, inp, wx, bias, far=5, us=20,
    )
    weights, driven = call(drive_kernel, driven, [inp32, stack], inp, wx, bias, weights, part, us=0.01, same={3: 0, 4: 1})
    (main,) = call(main_kernel, [((4 * ch, 128), BF16)], [], hid, us=0.01)
    n = lax.axis_size("lon")
    came_left = lax.ppermute(to_right, "lon", [(i, (i + 1) % n) for i in range(n)])
    came_right = lax.ppermute(to_left, "lon", [((i + 1) % n, i) for i in range(n)])
    from_right, from_left, strip = call(
        strip_kernel, [(to_left.shape, F32), (to_left.shape, F32), ((2 * FOLD, 128), BF16)], [],
        came_left, came_right, to_right, to_left,
    )
    shards = lax.axis_size("chan")
    paired = shards == 4 and 2 * ch == 128

    def others(x):
        return [lax.ppermute(x, "chan", [(i, i ^ k) for i in range(shards)]) for k in (1, 2)]

    def onward(same, before):
        (same,) = call(after_kernel, [(same.shape, BF16)], [], same, before, us=0.01)
        return same, lax.ppermute(same, "chan", [(i, i ^ 1) for i in range(shards)])

    field = main
    traveling = [lax.ppermute(field, "chan", [(i, i ^ k) for i in range(shards)]) for k in (1, 2, 3)] if paired else None
    blocks = [strip, *[lax.ppermute(strip, "chan", [(i, i ^ k) for i in range(shards)]) for k in (1, 2, 3)]] if paired else [lax.all_gather(strip, "chan", axis=0)]
    for step in range(STEPS):
        last = step == STEPS - 1
        hid32 = ((4 * ch, 128), F32)
        pre = ((4, gate, 128), F32)
        outs = [((4 * ch, 128), BF16), ((4 * ch, 128), F32)]
        rim = None
        if paired:
            other, same, *cross = traveling
            windowed = ((5, 2 * ch, 768), BF16)
            (part,) = call(near_kernel, [pre], [windowed], field, other, driven, w_hidden, us=0.01)
            if cross:
                (cross,) = cross
            else:
                (split,) = call(
                    split_kernel, [((2, 5 * len(SETS), gate, 128), BF16)], [], w_hidden, part, us=0.01
                )
                same, cross = onward(same, split)
        if not last:
            rim = call(
                rim_drive_kernel, [((gate, 128), F32)], [((padded(25 * cin), 128), BF16), inp32],
                from_right, from_left, inp, weights, *([part] if paired else []), us=0.01,
            )
        if paired and last:
            (part,) = call(
                functools.partial(shard_kernel, step, 0), [pre], [((5, ch, 768), BF16)],
                same, part, split, us=0.01,
            )
            field, cell = call(
                functools.partial(shard_kernel, step, 1), outs, [((5, ch, 768), BF16), pre, hid32],
                cross, part, split, cell, us=0.01,
            )
        elif paired:
            field, cell = call(
                functools.partial(far_kernel, step), outs, [windowed, pre, hid32],
                same, cross, part, cell, w_hidden, *(rim or []), us=0.01,
            )
        else:
            gathered = lax.all_gather(field, "chan", axis=0)
            field, cell = call(
                functools.partial(whole_kernel, step), outs,
                [((5, depth, 768), BF16), pre, hid32], gathered, driven, cell, w_hidden, us=3,
            )
        if not last:
            field, cell = call(
                rim_kernel, [((4 * ch + FOLD, 128), BF16), ((4 * ch, 128), F32)], [((1, gate, 128), F32)],
                *blocks, *rim, field, cell,
                to_right, to_left, from_right, from_left, w_hidden, us=0.01,
            )
            traveling = others(field) if paired else None
            (driven,) = call(
                functools.partial(next_drive_kernel, step + 1), [pre], [stack, inp32],
                from_right, from_left, inp, weights, field, us=0.01,
            )
    return field.reshape(ch, rows, cols), cell.reshape(ch, rows, cols)


def solution(mesh):
    in_specs = (
        P(None, None, "groups", "lon"),
        P("chan", "groups", "lon"),
        P("chan", "groups", "lon"),
        P(None, None, "chan", None),
        P(None, None, "chan", None),
        P("chan"),
    )
    out_specs = (P("chan", "groups", "lon"), P("chan", "groups", "lon"))
    return jax.shard_map(shards, mesh=mesh, in_specs=in_specs, out_specs=out_specs, check_vma=False)
```

```python
import functools

import jax
import jax.numpy as jnp
from jax import lax
from jax.experimental import pallas as pl
from jax.experimental.pallas import tpu as pltpu
from jax.sharding import PartitionSpec as P

STEPS = 2
FOLD = 16
F32, BF16 = jnp.float32, jnp.bfloat16


def lanes(rows):
    return lax.broadcasted_iota(jnp.int32, (rows, 128), 1)


def roll(x, by):
    by = by % 128
    return pltpu.roll(x, by, 1) if by else x


def unfold(block, channels):
    return jnp.concatenate(
        [roll(block[8 * (i // 4) : 8 * (i // 4) + 8], -32 * (i % 4)) for i in range(channels // 8)], axis=0
    )


def fold(field):
    lane = lanes(8)
    parts = [jnp.zeros((8, 128), F32) for _ in range(FOLD // 8)]
    for i in range(field.shape[0] // 8):
        base = 32 * (i % 4)
        here = (lane >= base) & (lane < base + 32)
        parts[i // 4] = jnp.where(here, roll(field[8 * i : 8 * i + 8], base), parts[i // 4])
    return jnp.concatenate(parts, axis=0)


def edges_of(rows, groups, vectors):
    lane = lanes(8)
    left = [jnp.zeros((8, 128), F32) for _ in range(vectors)]
    right = [jnp.zeros((8, 128), F32) for _ in range(vectors)]
    for i in range(groups):
        for y in range(4):
            base = 32 * (i % 4) + 8 * y
            moved = roll(rows(i, y), base + 4)
            left[i // 4] = jnp.where((lane >= base + 4) & (lane < base + 8), moved, left[i // 4])
            right[i // 4] = jnp.where((lane >= base) & (lane < base + 4), moved, right[i // 4])
    return jnp.concatenate(left, axis=0), jnp.concatenate(right, axis=0)


def pack_kernel(*refs):
    fars, (to_right, to_left, hid_out, weights, part) = refs[:5], refs[5:10]
    hid, cell, inp, wx, bias, hid32, inp32, xi, arrived = refs[10:]
    ch = hid.shape[0] // 4
    pairs = tuple(zip(fars, (hid, cell, inp, wx, bias)))
    copies = [pltpu.make_async_copy(a, b, arrived.at[i]) for i, (a, b) in enumerate(pairs)]
    for copy in copies:
        copy.start()
    copies[0].wait()
    hid32[...] = hid[...].astype(F32)
    hl, hr = edges_of(lambda i, y: hid32[pl.ds(32 * i + y, 8, stride=4), :], ch // 8, 2)
    hid_out[...] = hid32[...]
    copies[1].wait()
    cl, cr = edges_of(lambda i, y: cell[pl.ds(32 * i + y, 8, stride=4), :], ch // 8, 2)
    to_left[0:FOLD] = hl + roll(cl, -4)
    to_right[0:FOLD] = hr + roll(cr, 4)
    copies[2].wait()
    inp32[...] = inp[...].astype(F32)
    il, ir = edges_of(lambda i, y: inp32[pl.ds(32 * i + y, 8, stride=4), :], inp.shape[0] // 32, 1)
    to_left[FOLD:] = il
    to_right[FOLD:] = ir
    for copy in copies[3:]:
        copy.wait()

    @pl.when(lax.axis_index("lon") == 0)
    def _():
        drive(inp, inp32, wx, bias, weights, part, xi)


def main_kernel(hid, main):
    ch = hid.shape[0] // 4
    for y in range(4):
        main[y * ch : (y + 1) * ch, :] = hid[pl.ds(y, ch, stride=4), :].astype(BF16)


def strip_kernel(came_left, came_right, to_right, to_left, from_right, from_left, out):
    from_left[...], from_right[...] = came_left[...], came_right[...]
    low = (lanes(FOLD) & 7) < 4
    out[0:FOLD] = jnp.where(low, from_left[0:FOLD], from_right[0:FOLD]).astype(BF16)
    out[FOLD:] = jnp.where(low, to_right[0:FOLD], to_left[0:FOLD]).astype(BF16)


def windows(row, halo, y):
    if halo is None:
        return [roll(row, -d) for d in range(-2, 3)]
    lane = lanes(row.shape[0])
    ring = roll(halo, -(8 * y + 4))
    out = []
    for d in range(-2, 3):
        if d == 0:
            out.append(row)
        else:
            other = lane >= 128 + d if d < 0 else lane < d
            out.append(roll(jnp.where(other, ring, row), -d))
    return out


def strips(halo, own):
    lane = lanes(halo.shape[0])
    low, left, used = (lane & 7) < 4, lane < 64, lane < 32
    halo, own = [jnp.where(used, x, jnp.zeros_like(x)) for x in (halo, own)]
    return jnp.where(
        left, jnp.where(low, roll(halo, 16), roll(own, 16)), jnp.where(low, roll(own, 80), roll(halo, 80))
    )


def own_edges(rows):
    lane = lanes(rows[0].shape[0])
    own = jnp.zeros_like(rows[0])
    for y in range(4):
        own = jnp.where((lane >= 8 * y) & (lane < 8 * y + 8), roll(rows[y], 8 * y + 4), own)
    return own


def sigmoid(x):
    return 0.5 * jnp.tanh(0.5 * x) + 0.5


def gates(pre, ch, at, cell):
    part = [pre[at, pl.ds(g, ch, stride=4), :] for g in range(4)]
    cell = sigmoid(part[1]) * cell + sigmoid(part[0]) * jnp.tanh(part[2])
    return sigmoid(part[3]) * jnp.tanh(cell), cell


def near_far(own, other, ch):
    return rows_of(ordered(own, other), ch)


def rows_of(shards, ch):
    rows = [jnp.concatenate([s[y * ch : (y + 1) * ch] for s in shards], axis=0) for y in range(4)]
    if shards[0].shape[0] == 4 * ch:
        return rows, None
    halo = jnp.concatenate([unfold(s[4 * ch : 4 * ch + FOLD].astype(F32), ch) for s in shards], axis=0)
    return rows, halo.astype(BF16)


def store_windows(xs, rows, halo):
    depth = rows[0].shape[0]
    for b in range(5):
        xs[b, :, 0:128] = jnp.zeros((depth, 128), BF16)
        xs[b, :, 640:768] = jnp.zeros((depth, 128), BF16)
    for y in range(4):
        for b, window in enumerate(windows(rows[y], halo, y)):
            xs[b, :, 128 * (y + 1) : 128 * (y + 2)] = window


def hidden_rows(w, xs, at, pair):
    depth = xs.shape[1]
    terms = [(a, b, 2 * pair + a - 2) for a in range(5) for b in range(5) if -2 < 2 * pair + a - 2 < 4]
    left = jnp.concatenate([w[a, b, :, pl.ds(at, depth)] for a, b, _ in terms], axis=1)
    right = jnp.concatenate([xs[b, :, 128 * (lo + 1) : 128 * (lo + 3)] for _, b, lo in terms], axis=0)
    return jnp.dot(left, right, preferred_element_type=F32)


def hidden_rim(w, strip, at):
    stack = jnp.concatenate([roll(strip, -8 * (a - 2)) for a in range(5)], axis=0)
    total = None
    for b in range(5):
        left = jnp.concatenate([w[a, b, :, pl.ds(at, strip.shape[0])] for a in range(5)], axis=1)
        part = roll(jnp.dot(left, stack, preferred_element_type=F32), -(b - 2))
        total = part if total is None else total + part
    return total


def input_rows(step, inp32, inp, from_right, from_left):
    cin = inp.shape[0] // (4 * STEPS)
    inp32[...] = inp[...].astype(F32)
    rows = [inp32[pl.ds(4 * cin * step + y, cin, stride=4), :].astype(BF16) for y in range(4)]
    low = (lanes(8) & 7) < 4
    block = jnp.where(low, from_left[FOLD:], from_right[FOLD:])
    first = step * cin // 8
    halo = jnp.concatenate([roll(block, -32 * i) for i in range(first, first + cin // 8)], axis=0).astype(BF16)
    return rows, halo


def store_inputs(xi, rows, halo):
    cin = rows[0].shape[0]
    wins = [windows(rows[y], halo, y) for y in range(4)]
    for a in range(5):
        for b in range(5):
            at = cin * (5 * a + b)
            for y in range(4):
                r = y + a - 2
                xi[at : at + cin, 128 * y : 128 * (y + 1)] = (
                    wins[r][b] if 0 <= r < 4 else jnp.zeros((cin, 128), BF16)
                )
    store_ones(xi, 25 * cin)


def store_input_rim(xi, rows, halo):
    cin = halo.shape[0]
    strip = strips(halo, own_edges(rows))
    for a in range(5):
        for b in range(5):
            at = cin * (5 * a + b)
            xi[at : at + cin, :] = roll(strip, -(8 * (a - 2) + b - 2))
    store_ones(xi, 25 * cin)


def store_ones(xi, taps):
    ones = lax.broadcasted_iota(jnp.int32, (16, xi.shape[1]), 0) < 3
    xi[taps : taps + 16, :] = jnp.where(ones, 1.0, 0.0).astype(BF16)
    xi[taps + 16 :, :] = jnp.zeros((xi.shape[0] - taps - 16, xi.shape[1]), BF16)


def input_weights(wx, bias):
    taps, gate = wx.shape
    b0 = bias[...]
    b1 = b0.astype(BF16).astype(F32)
    b2 = (b0 - b1).astype(BF16).astype(F32)
    b3 = b0 - b1 - b2
    sub = lax.broadcasted_iota(jnp.int32, (16, gate), 0)
    extra = jnp.where(sub == 0, b1, jnp.where(sub == 1, b2, jnp.where(sub == 2, b3, 0.0)))
    blank = jnp.zeros((padded(taps) - taps - 16, gate), F32)
    return jnp.concatenate([wx[...].astype(F32), extra, blank], axis=0).T.astype(BF16)


def padded(taps):
    return (taps + 16 + 127) // 128 * 128


def drive(inp, inp32, wx, bias, weights, part, xi):
    cin = inp.shape[0] // (4 * STEPS)
    inp32[...] = inp[...].astype(F32)
    weights[...] = input_weights(wx, bias)
    store_inputs(xi, [inp32[pl.ds(y, cin, stride=4), :].astype(BF16) for y in range(4)], None)
    for pair in range(2):
        total = input_part(weights, xi, 256 * pair, 256)
        part[2 * pair] = total[:, 0:128]
        part[2 * pair + 1] = total[:, 128:256]


def drive_kernel(inp, wx, bias, weights_in, part_in, weights, part, inp32, xi):
    @pl.when(lax.axis_index("lon") != 0)
    def _():
        drive(inp, inp32, wx, bias, weights, part, xi)


def input_part(weights, xi, at, wide):
    return jnp.dot(weights[...], xi[:, at : at + wide], preferred_element_type=F32)


def rim_gates(pre, to_right, to_left, from_right, from_left, ch):
    low = (lanes(FOLD) & 7) < 4
    halo = unfold(jnp.where(low, from_right[0:FOLD], from_left[0:FOLD]), ch)
    own = unfold(jnp.where(low, to_left[0:FOLD], to_right[0:FOLD]), ch)
    halo, own = [jnp.where((lanes(ch) & 7) < 4, roll(x, -4), roll(x, 4)) for x in (halo, own)]
    return gates(pre, ch, 0, strips(halo, own))


def rim_fold(h):
    h = jnp.where((lanes(h.shape[0]) & 7) < 4, roll(h, -16), roll(h, -80))
    return fold(h).astype(BF16)


def patch(row, rim, y):
    lane = lanes(row.shape[0])
    base = 8 * y + 16
    row = jnp.where(lane < 2, roll(rim, -(base + 4)), row)
    return jnp.where(lane >= 126, roll(rim, 60 - base), row)


def finish(step, pre, cell, hid_out, cell_out, hid32):
    ch = cell.shape[0] // 4
    last = step == STEPS - 1
    for y in range(4):
        before = cell[pl.ds(y, ch, stride=4), :] if step == 0 else cell[y * ch : (y + 1) * ch, :]
        h, c = gates(pre, ch, y, before)
        if last:
            cell_out[pl.ds(y, ch, stride=4), :] = c
            hid32[pl.ds(y, ch, stride=4), :] = h
        else:
            cell_out[y * ch : (y + 1) * ch, :] = c
            hid_out[y * ch : (y + 1) * ch, :] = h.astype(BF16)
    if last:
        hid_out[...] = hid32[...].astype(BF16)


def whole_kernel(step, gathered, driven, cell, w, hid_out, cell_out, xs, pre, hid32):
    shards, ch = gathered.shape[0], cell.shape[0] // 4
    store_windows(xs, *rows_of([gathered[c] for c in range(shards)], ch))
    for pair in range(2):
        total = hidden_rows(w, xs, 0, pair)
        pre[2 * pair] = driven[2 * pair] + total[:, 0:128]
        pre[2 * pair + 1] = driven[2 * pair + 1] + total[:, 128:256]
    finish(step, pre, cell, hid_out, cell_out, hid32)


def first_channel(depth, remote):
    mine = lax.axis_index("chan") // 2
    return pl.multiple_of((1 - mine if remote else mine) * depth, depth)


def after_kernel(x, before, out):
    out[...] = x[...]


def near_kernel(own, other, driven, w, part, xs):
    ch = w.shape[2] // 4
    at = first_channel(2 * ch, False)
    store_windows(xs, *near_far(own, other, ch))
    for pair in range(2):
        total = hidden_rows(w, xs, at, pair)
        part[2 * pair] = driven[2 * pair] + total[:, 0:128]
        part[2 * pair + 1] = driven[2 * pair + 1] + total[:, 128:256]


def next_drive_kernel(step, from_right, from_left, inp, weights, before, part, xi, inp32):
    store_inputs(xi, *input_rows(step, inp32, inp, from_right, from_left))
    for pair in range(2):
        total = input_part(weights, xi, 256 * pair, 256)
        part[2 * pair] = total[:, 0:128]
        part[2 * pair + 1] = total[:, 128:256]


def far_kernel(step, same, cross, part, cell, w, *refs):
    ch = cell.shape[0] // 4
    hid_out, cell_out, xs, pre, hid32 = refs[-5:]
    at = first_channel(2 * ch, True)
    store_windows(xs, *near_far(same, cross, ch))
    for pair in range(2):
        total = hidden_rows(w, xs, at, pair)
        pre[2 * pair] = part[2 * pair] + total[:, 0:128]
        pre[2 * pair + 1] = part[2 * pair + 1] + total[:, 128:256]
    finish(step, pre, cell, hid_out, cell_out, hid32)


SETS = ((1, 2), (3, 4), (0, 3))


def split_kernel(w, before, out):
    half = w.shape[3] // 4
    at = first_channel(2 * half, True)
    even = lax.axis_index("chan") % 2 == 0
    left = lanes(w.shape[2]) < half
    for k, (one, two) in enumerate(SETS):
        for b in range(5):
            x, y = w[one, b, :, pl.ds(at, 2 * half)], w[two, b, :, pl.ds(at, 2 * half)]
            low, high = jnp.where(left, x, roll(y, half)), jnp.where(left, roll(x, half), y)
            out[0, 5 * k + b] = jnp.where(even, low, high)
            out[1, 5 * k + b] = jnp.where(even, high, low)


def shard_rows(weights, which, xs, pair):
    left, right = [], []
    for k in (0, pair + 1):
        for b in range(5):
            left.append(weights[which, 5 * k + b])
            for a in SETS[k]:
                lo = 2 * pair + a - 2
                right.append(xs[b, :, 128 * (lo + 1) : 128 * (lo + 3)])
    return jnp.dot(jnp.concatenate(left, axis=1), jnp.concatenate(right, axis=0), preferred_element_type=F32)


def shard_kernel(step, which, shard, part, weights, *refs):
    if which == 0:
        pre, xs = refs
    else:
        *ends, xs, pre = (*refs[:3], *refs[5:], *refs[3:5])
    ch = shard.shape[0] // 4 - FOLD // 4
    store_windows(xs, *rows_of([shard[...]], ch))
    for pair in range(2):
        total = shard_rows(weights, which, xs, pair)
        pre[2 * pair] = part[2 * pair] + total[:, 0:128]
        pre[2 * pair + 1] = part[2 * pair + 1] + total[:, 128:256]
    if which == 1:
        cell, hid_out, cell_out, hid32, cell32, hid16, sent = ends
        for y in range(4):
            part = [pre[y, pl.ds(g, ch, stride=4), :] for g in range(3)]
            c = sigmoid(part[1]) * cell[y * ch : (y + 1) * ch, :] + sigmoid(part[0]) * jnp.tanh(part[2])
            cell32[pl.ds(y, ch, stride=4), :] = c
        copy = pltpu.make_async_copy(cell32, cell_out, sent.at[0])
        copy.start()
        for y in range(4):
            c = cell32[pl.ds(y, ch, stride=4), :]
            hid32[pl.ds(y, ch, stride=4), :] = sigmoid(pre[y, pl.ds(3, ch, stride=4), :]) * jnp.tanh(c)
        hid16[...] = hid32[...].astype(BF16)
        other = pltpu.make_async_copy(hid16, hid_out, sent.at[1])
        other.start()
        copy.wait()
        other.wait()


def rim_strips(shards, ch):
    halo = jnp.concatenate([unfold(s[0:FOLD].astype(F32), ch) for s in shards], axis=0).astype(BF16)
    own = jnp.concatenate([unfold(s[FOLD:].astype(F32), ch) for s in shards], axis=0).astype(BF16)
    return strips(halo, own)


def ordered(own, other):
    even = lax.axis_index("chan") % 2 == 0
    return [jnp.where(even, own[...], other[...]), jnp.where(even, other[...], own[...])]


def rim_drive_kernel(from_right, from_left, inp, weights, *refs):
    part, xi, inp32 = refs[-3:]
    store_input_rim(xi, *input_rows(0, inp32, inp, from_right, from_left))
    part[...] = input_part(weights, xi, 0, 128)


def rim_kernel(*refs):
    *blocks, part, hid, cell, to_right, to_left, from_right, from_left, w, hid_out, cell_out, pre = refs
    ch = cell.shape[0] // 4
    if len(blocks) == 4:
        first = lax.axis_index("chan") // 2 == 0
        here, there = ordered(*blocks[:2]), ordered(*blocks[2:])
        shards = [jnp.where(first, here[k], there[k]) for k in (0, 1)]
        shards += [jnp.where(first, there[k], here[k]) for k in (0, 1)]
    else:
        shards = [blocks[0][c] for c in range(blocks[0].shape[0])]
    pre[0] = part[...] + hidden_rim(w, rim_strips(shards, ch), 0)
    h, c = rim_gates(pre, to_right, to_left, from_right, from_left, ch)
    for y in range(4):
        at = slice(y * ch, (y + 1) * ch)
        hid_out[at, :] = patch(hid[at, :].astype(F32), h, y).astype(BF16)
        cell_out[at, :] = patch(cell[at, :], c, y)
    hid_out[4 * ch : 4 * ch + FOLD, :] = rim_fold(h)


def call(kernel, outs, scratch, *args, far=0, us=1, same=None, kept=0):
    return pl.pallas_call(
        kernel,
        out_shape=[jax.ShapeDtypeStruct(s, d) for s, d in outs],
        in_specs=[pl.BlockSpec(memory_space=pltpu.HBM)] * far
        + [pl.BlockSpec(memory_space=pltpu.VMEM)] * (len(args) - far),
        out_specs=[pl.BlockSpec(memory_space=pltpu.VMEM)] * (len(outs) - kept)
        + [pl.BlockSpec(memory_space=pltpu.HBM)] * kept,
        scratch_shapes=[pltpu.VMEM(s, d) for s, d in scratch] + ([pltpu.SemaphoreType.DMA((far + kept,))] if far + kept else []),
        input_output_aliases=same or {},
        cost_estimate=pl.CostEstimate(flops=int(us * 1e9), bytes_accessed=0, transcendentals=0),
        compiler_params=pltpu.CompilerParams(vmem_limit_bytes=24 << 20),
    )(*[pltpu.with_memory_space_constraint(a, pltpu.HBM) if i < far else a for i, a in enumerate(args)])


def shards(inputs, hidden_init, cell_init, w_input, w_hidden, gate_bias):
    ch, rows, cols = hidden_init.shape
    gate = 4 * ch
    depth = w_hidden.shape[3]
    cin = w_input.shape[3]
    hid = hidden_init.reshape(ch * rows, cols)
    cell = cell_init.reshape(ch * rows, cols)
    inp = inputs.reshape(-1, cols)
    wx = jnp.transpose(w_input, (0, 1, 3, 2)).reshape(25 * cin, gate)
    bias = gate_bias.reshape(1, gate)
    driven = [((gate, padded(25 * cin)), BF16), ((4, gate, 128), F32)]
    stack = ((padded(25 * cin), 512), BF16)
    inp32 = (inp.shape, F32)
    to_right, to_left, hid, weights, part = call(
        pack_kernel,
        [((FOLD + 8, 128), F32), ((FOLD + 8, 128), F32), ((4 * ch, 128), F32), *driven],
        [(hid.shape, BF16), (cell.shape, F32), (inp.shape, BF16), (wx.shape, BF16), (bias.shape, F32),
         (hid.shape, F32), inp32, stack],
        hid, cell, inp, wx, bias, far=5, us=20,
    )
    weights, driven = call(drive_kernel, driven, [inp32, stack], inp, wx, bias, weights, part, us=0.01, same={3: 0, 4: 1})
    (main,) = call(main_kernel, [((4 * ch, 128), BF16)], [], hid, us=0.01)
    n = lax.axis_size("lon")
    came_left = lax.ppermute(to_right, "lon", [(i, (i + 1) % n) for i in range(n)])
    came_right = lax.ppermute(to_left, "lon", [((i + 1) % n, i) for i in range(n)])
    from_right, from_left, strip = call(
        strip_kernel, [(to_left.shape, F32), (to_left.shape, F32), ((2 * FOLD, 128), BF16)], [],
        came_left, came_right, to_right, to_left,
    )
    shards = lax.axis_size("chan")
    paired = shards == 4 and 2 * ch == 128

    def others(x):
        return [lax.ppermute(x, "chan", [(i, i ^ k) for i in range(shards)]) for k in (1, 2)]

    def onward(same, before):
        (same,) = call(after_kernel, [(same.shape, BF16)], [], same, before, us=0.01)
        return same, lax.ppermute(same, "chan", [(i, i ^ 1) for i in range(shards)])

    field = main
    traveling = [lax.ppermute(field, "chan", [(i, i ^ k) for i in range(shards)]) for k in (1, 2, 3)] if paired else None
    blocks = [strip, *[lax.ppermute(strip, "chan", [(i, i ^ k) for i in range(shards)]) for k in (1, 2, 3)]] if paired else [lax.all_gather(strip, "chan", axis=0)]
    for step in range(STEPS):
        last = step == STEPS - 1
        hid32 = ((4 * ch, 128), F32)
        pre = ((4, gate, 128), F32)
        outs = [((4 * ch, 128), BF16), ((4 * ch, 128), F32)]
        rim = None
        if paired:
            other, same, *cross = traveling
            windowed = ((5, 2 * ch, 768), BF16)
            (part,) = call(near_kernel, [pre], [windowed], field, other, driven, w_hidden, us=0.01)
            if cross:
                (cross,) = cross
            else:
                (split,) = call(
                    split_kernel, [((2, 5 * len(SETS), gate, 128), BF16)], [], w_hidden, part, us=0.01
                )
                same, cross = onward(same, split)
        if not last:
            rim = call(
                rim_drive_kernel, [((gate, 128), F32)], [((padded(25 * cin), 128), BF16), inp32],
                from_right, from_left, inp, weights, *([part] if paired else []), us=0.01,
            )
        if paired and last:
            (part,) = call(
                functools.partial(shard_kernel, step, 0), [pre], [((5, ch, 768), BF16)],
                same, part, split, us=0.01,
            )
            field, cell = call(
                functools.partial(shard_kernel, step, 1), outs,
                [((5, ch, 768), BF16), pre, hid32, hid32, ((4 * ch, 128), BF16)], cross, part, split, cell,
                us=0.01, kept=2,
            )
        elif paired:
            field, cell = call(
                functools.partial(far_kernel, step), outs, [windowed, pre, hid32],
                same, cross, part, cell, w_hidden, *(rim or []), us=0.01,
            )
        else:
            gathered = lax.all_gather(field, "chan", axis=0)
            field, cell = call(
                functools.partial(whole_kernel, step), outs,
                [((5, depth, 768), BF16), pre, hid32], gathered, driven, cell, w_hidden, us=3,
            )
        if not last:
            field, cell = call(
                rim_kernel, [((4 * ch + FOLD, 128), BF16), ((4 * ch, 128), F32)], [((1, gate, 128), F32)],
                *blocks, *rim, field, cell,
                to_right, to_left, from_right, from_left, w_hidden, us=0.01,
            )
            traveling = others(field) if paired else None
            (driven,) = call(
                functools.partial(next_drive_kernel, step + 1), [pre], [stack, inp32],
                from_right, from_left, inp, weights, field, us=0.01,
            )
    return field.reshape(ch, rows, cols), cell.reshape(ch, rows, cols)


def solution(mesh):
    in_specs = (
        P(None, None, "groups", "lon"),
        P("chan", "groups", "lon"),
        P("chan", "groups", "lon"),
        P(None, None, "chan", None),
        P(None, None, "chan", None),
        P("chan"),
    )
    out_specs = (P("chan", "groups", "lon"), P("chan", "groups", "lon"))
    return jax.shard_map(shards, mesh=mesh, in_specs=in_specs, out_specs=out_specs, check_vma=False)
```

```python
import functools

import jax
import jax.numpy as jnp
from jax import lax
from jax.experimental import pallas as pl
from jax.experimental.pallas import tpu as pltpu
from jax.sharding import PartitionSpec as P

STEPS = 2
FOLD = 16
F32, BF16 = jnp.float32, jnp.bfloat16


def lanes(rows):
    return lax.broadcasted_iota(jnp.int32, (rows, 128), 1)


def roll(x, by):
    by = by % 128
    return pltpu.roll(x, by, 1) if by else x


def unfold(block, channels):
    return jnp.concatenate(
        [roll(block[8 * (i // 4) : 8 * (i // 4) + 8], -32 * (i % 4)) for i in range(channels // 8)], axis=0
    )


def fold(field):
    lane = lanes(8)
    parts = [jnp.zeros((8, 128), F32) for _ in range(FOLD // 8)]
    for i in range(field.shape[0] // 8):
        base = 32 * (i % 4)
        here = (lane >= base) & (lane < base + 32)
        parts[i // 4] = jnp.where(here, roll(field[8 * i : 8 * i + 8], base), parts[i // 4])
    return jnp.concatenate(parts, axis=0)


def edges_of(rows, groups, vectors):
    lane = lanes(8)
    left = [jnp.zeros((8, 128), F32) for _ in range(vectors)]
    right = [jnp.zeros((8, 128), F32) for _ in range(vectors)]
    for i in range(groups):
        for y in range(4):
            base = 32 * (i % 4) + 8 * y
            moved = roll(rows(i, y), base + 4)
            left[i // 4] = jnp.where((lane >= base + 4) & (lane < base + 8), moved, left[i // 4])
            right[i // 4] = jnp.where((lane >= base) & (lane < base + 4), moved, right[i // 4])
    return jnp.concatenate(left, axis=0), jnp.concatenate(right, axis=0)


def pack_kernel(*refs):
    fars, (to_right, to_left, hid_out, weights, part) = refs[:5], refs[5:10]
    hid, cell, inp, wx, bias, hid32, inp32, xi, arrived = refs[10:]
    ch = hid.shape[0] // 4
    pairs = tuple(zip(fars, (hid, cell, inp, wx, bias)))
    copies = [pltpu.make_async_copy(a, b, arrived.at[i]) for i, (a, b) in enumerate(pairs)]
    for copy in copies:
        copy.start()
    for copy in copies:
        copy.wait()
    hid32[...] = hid[...].astype(F32)
    inp32[...] = inp[...].astype(F32)
    hl, hr = edges_of(lambda i, y: hid32[pl.ds(32 * i + y, 8, stride=4), :], ch // 8, 2)
    cl, cr = edges_of(lambda i, y: cell[pl.ds(32 * i + y, 8, stride=4), :], ch // 8, 2)
    il, ir = edges_of(lambda i, y: inp32[pl.ds(32 * i + y, 8, stride=4), :], inp.shape[0] // 32, 1)
    to_left[0:FOLD] = hl + roll(cl, -4)
    to_left[FOLD:] = il
    to_right[0:FOLD] = hr + roll(cr, 4)
    to_right[FOLD:] = ir
    hid_out[...] = hid32[...]

    @pl.when(lax.axis_index("lon") == 0)
    def _():
        drive(inp, inp32, wx, bias, weights, part, xi)


def main_kernel(hid, main):
    ch = hid.shape[0] // 4
    for y in range(4):
        main[y * ch : (y + 1) * ch, :] = hid[pl.ds(y, ch, stride=4), :].astype(BF16)


def strip_kernel(came_left, came_right, to_right, to_left, from_right, from_left, out):
    from_left[...], from_right[...] = came_left[...], came_right[...]
    low = (lanes(FOLD) & 7) < 4
    out[0:FOLD] = jnp.where(low, from_left[0:FOLD], from_right[0:FOLD]).astype(BF16)
    out[FOLD:] = jnp.where(low, to_right[0:FOLD], to_left[0:FOLD]).astype(BF16)


def windows(row, halo, y):
    if halo is None:
        return [roll(row, -d) for d in range(-2, 3)]
    lane = lanes(row.shape[0])
    ring = roll(halo, -(8 * y + 4))
    out = []
    for d in range(-2, 3):
        if d == 0:
            out.append(row)
        else:
            other = lane >= 128 + d if d < 0 else lane < d
            out.append(roll(jnp.where(other, ring, row), -d))
    return out


def strips(halo, own):
    lane = lanes(halo.shape[0])
    low, left, used = (lane & 7) < 4, lane < 64, lane < 32
    halo, own = [jnp.where(used, x, jnp.zeros_like(x)) for x in (halo, own)]
    return jnp.where(
        left, jnp.where(low, roll(halo, 16), roll(own, 16)), jnp.where(low, roll(own, 80), roll(halo, 80))
    )


def own_edges(rows):
    lane = lanes(rows[0].shape[0])
    own = jnp.zeros_like(rows[0])
    for y in range(4):
        own = jnp.where((lane >= 8 * y) & (lane < 8 * y + 8), roll(rows[y], 8 * y + 4), own)
    return own


def sigmoid(x):
    return 0.5 * jnp.tanh(0.5 * x) + 0.5


def gates(pre, ch, at, cell):
    part = [pre[at, pl.ds(g, ch, stride=4), :] for g in range(4)]
    cell = sigmoid(part[1]) * cell + sigmoid(part[0]) * jnp.tanh(part[2])
    return sigmoid(part[3]) * jnp.tanh(cell), cell


def near_far(own, other, ch):
    return rows_of(ordered(own, other), ch)


def rows_of(shards, ch):
    rows = [jnp.concatenate([s[y * ch : (y + 1) * ch] for s in shards], axis=0) for y in range(4)]
    if shards[0].shape[0] == 4 * ch:
        return rows, None
    halo = jnp.concatenate([unfold(s[4 * ch : 4 * ch + FOLD].astype(F32), ch) for s in shards], axis=0)
    return rows, halo.astype(BF16)


def store_windows(xs, rows, halo):
    depth = rows[0].shape[0]
    for b in range(5):
        xs[b, :, 0:128] = jnp.zeros((depth, 128), BF16)
        xs[b, :, 640:768] = jnp.zeros((depth, 128), BF16)
    for y in range(4):
        for b, window in enumerate(windows(rows[y], halo, y)):
            xs[b, :, 128 * (y + 1) : 128 * (y + 2)] = window


def hidden_rows(w, xs, at, pair):
    depth = xs.shape[1]
    terms = [(a, b, 2 * pair + a - 2) for a in range(5) for b in range(5) if -2 < 2 * pair + a - 2 < 4]
    left = jnp.concatenate([w[a, b, :, pl.ds(at, depth)] for a, b, _ in terms], axis=1)
    right = jnp.concatenate([xs[b, :, 128 * (lo + 1) : 128 * (lo + 3)] for _, b, lo in terms], axis=0)
    return jnp.dot(left, right, preferred_element_type=F32)


def hidden_rim(w, strip, at):
    stack = jnp.concatenate([roll(strip, -8 * (a - 2)) for a in range(5)], axis=0)
    total = None
    for b in range(5):
        left = jnp.concatenate([w[a, b, :, pl.ds(at, strip.shape[0])] for a in range(5)], axis=1)
        part = roll(jnp.dot(left, stack, preferred_element_type=F32), -(b - 2))
        total = part if total is None else total + part
    return total


def input_rows(step, inp32, inp, from_right, from_left):
    cin = inp.shape[0] // (4 * STEPS)
    inp32[...] = inp[...].astype(F32)
    rows = [inp32[pl.ds(4 * cin * step + y, cin, stride=4), :].astype(BF16) for y in range(4)]
    low = (lanes(8) & 7) < 4
    block = jnp.where(low, from_left[FOLD:], from_right[FOLD:])
    first = step * cin // 8
    halo = jnp.concatenate([roll(block, -32 * i) for i in range(first, first + cin // 8)], axis=0).astype(BF16)
    return rows, halo


def store_inputs(xi, rows, halo):
    cin = rows[0].shape[0]
    wins = [windows(rows[y], halo, y) for y in range(4)]
    for a in range(5):
        for b in range(5):
            at = cin * (5 * a + b)
            for y in range(4):
                r = y + a - 2
                xi[at : at + cin, 128 * y : 128 * (y + 1)] = (
                    wins[r][b] if 0 <= r < 4 else jnp.zeros((cin, 128), BF16)
                )
    store_ones(xi, 25 * cin)


def store_input_rim(xi, rows, halo):
    cin = halo.shape[0]
    strip = strips(halo, own_edges(rows))
    for a in range(5):
        for b in range(5):
            at = cin * (5 * a + b)
            xi[at : at + cin, :] = roll(strip, -(8 * (a - 2) + b - 2))
    store_ones(xi, 25 * cin)


def store_ones(xi, taps):
    ones = lax.broadcasted_iota(jnp.int32, (16, xi.shape[1]), 0) < 3
    xi[taps : taps + 16, :] = jnp.where(ones, 1.0, 0.0).astype(BF16)
    xi[taps + 16 :, :] = jnp.zeros((xi.shape[0] - taps - 16, xi.shape[1]), BF16)


def input_weights(wx, bias):
    taps, gate = wx.shape
    b0 = bias[...]
    b1 = b0.astype(BF16).astype(F32)
    b2 = (b0 - b1).astype(BF16).astype(F32)
    b3 = b0 - b1 - b2
    sub = lax.broadcasted_iota(jnp.int32, (16, gate), 0)
    extra = jnp.where(sub == 0, b1, jnp.where(sub == 1, b2, jnp.where(sub == 2, b3, 0.0)))
    blank = jnp.zeros((padded(taps) - taps - 16, gate), F32)
    return jnp.concatenate([wx[...].astype(F32), extra, blank], axis=0).T.astype(BF16)


def padded(taps):
    return (taps + 16 + 127) // 128 * 128


def drive(inp, inp32, wx, bias, weights, part, xi):
    cin = inp.shape[0] // (4 * STEPS)
    inp32[...] = inp[...].astype(F32)
    weights[...] = input_weights(wx, bias)
    store_inputs(xi, [inp32[pl.ds(y, cin, stride=4), :].astype(BF16) for y in range(4)], None)
    for pair in range(2):
        total = input_part(weights, xi, 256 * pair, 256)
        part[2 * pair] = total[:, 0:128]
        part[2 * pair + 1] = total[:, 128:256]


def drive_kernel(inp, wx, bias, weights_in, part_in, weights, part, inp32, xi):
    @pl.when(lax.axis_index("lon") != 0)
    def _():
        drive(inp, inp32, wx, bias, weights, part, xi)


def input_part(weights, xi, at, wide):
    return jnp.dot(weights[...], xi[:, at : at + wide], preferred_element_type=F32)


def rim_gates(pre, to_right, to_left, from_right, from_left, ch):
    low = (lanes(FOLD) & 7) < 4
    halo = unfold(jnp.where(low, from_right[0:FOLD], from_left[0:FOLD]), ch)
    own = unfold(jnp.where(low, to_left[0:FOLD], to_right[0:FOLD]), ch)
    halo, own = [jnp.where((lanes(ch) & 7) < 4, roll(x, -4), roll(x, 4)) for x in (halo, own)]
    return gates(pre, ch, 0, strips(halo, own))


def rim_fold(h):
    h = jnp.where((lanes(h.shape[0]) & 7) < 4, roll(h, -16), roll(h, -80))
    return fold(h).astype(BF16)


def patch(row, rim, y):
    lane = lanes(row.shape[0])
    base = 8 * y + 16
    row = jnp.where(lane < 2, roll(rim, -(base + 4)), row)
    return jnp.where(lane >= 126, roll(rim, 60 - base), row)


def finish(step, pre, cell, hid_out, cell_out, hid32):
    ch = cell.shape[0] // 4
    last = step == STEPS - 1
    for y in range(4):
        before = cell[pl.ds(y, ch, stride=4), :] if step == 0 else cell[y * ch : (y + 1) * ch, :]
        h, c = gates(pre, ch, y, before)
        if last:
            cell_out[pl.ds(y, ch, stride=4), :] = c
            hid32[pl.ds(y, ch, stride=4), :] = h
        else:
            cell_out[y * ch : (y + 1) * ch, :] = c
            hid_out[y * ch : (y + 1) * ch, :] = h.astype(BF16)
    if last:
        hid_out[...] = hid32[...].astype(BF16)


def whole_kernel(step, gathered, driven, cell, w, hid_out, cell_out, xs, pre, hid32):
    shards, ch = gathered.shape[0], cell.shape[0] // 4
    store_windows(xs, *rows_of([gathered[c] for c in range(shards)], ch))
    for pair in range(2):
        total = hidden_rows(w, xs, 0, pair)
        pre[2 * pair] = driven[2 * pair] + total[:, 0:128]
        pre[2 * pair + 1] = driven[2 * pair + 1] + total[:, 128:256]
    finish(step, pre, cell, hid_out, cell_out, hid32)


def first_channel(depth, remote):
    mine = lax.axis_index("chan") // 2
    return pl.multiple_of((1 - mine if remote else mine) * depth, depth)


def after_kernel(x, before, out):
    out[...] = x[...]


def near_kernel(own, other, driven, w, part, xs):
    ch = w.shape[2] // 4
    at = first_channel(2 * ch, False)
    store_windows(xs, *near_far(own, other, ch))
    for pair in range(2):
        total = hidden_rows(w, xs, at, pair)
        part[2 * pair] = driven[2 * pair] + total[:, 0:128]
        part[2 * pair + 1] = driven[2 * pair + 1] + total[:, 128:256]


def next_drive_kernel(step, from_right, from_left, inp, weights, before, part, xi, inp32):
    store_inputs(xi, *input_rows(step, inp32, inp, from_right, from_left))
    for pair in range(2):
        total = input_part(weights, xi, 256 * pair, 256)
        part[2 * pair] = total[:, 0:128]
        part[2 * pair + 1] = total[:, 128:256]


def far_kernel(step, cross, same, part, cell, w, *refs):
    ch = cell.shape[0] // 4
    hid_out, cell_out, xs, pre, hid32 = refs[-5:]
    at = first_channel(2 * ch, True)
    store_windows(xs, *near_far(same, cross, ch))
    for pair in range(2):
        total = hidden_rows(w, xs, at, pair)
        pre[2 * pair] = part[2 * pair] + total[:, 0:128]
        pre[2 * pair + 1] = part[2 * pair + 1] + total[:, 128:256]
    finish(step, pre, cell, hid_out, cell_out, hid32)


SETS = ((1, 2), (3, 4), (0, 3))


def split_kernel(w, before, out):
    half = w.shape[3] // 4
    at = first_channel(2 * half, True)
    even = lax.axis_index("chan") % 2 == 0
    left = lanes(w.shape[2]) < half
    for k, (one, two) in enumerate(SETS):
        for b in range(5):
            x, y = w[one, b, :, pl.ds(at, 2 * half)], w[two, b, :, pl.ds(at, 2 * half)]
            low, high = jnp.where(left, x, roll(y, half)), jnp.where(left, roll(x, half), y)
            out[0, 5 * k + b] = jnp.where(even, low, high)
            out[1, 5 * k + b] = jnp.where(even, high, low)


def shard_rows(weights, which, xs, pair):
    left, right = [], []
    for k in (0, pair + 1):
        for b in range(5):
            left.append(weights[which, 5 * k + b])
            for a in SETS[k]:
                lo = 2 * pair + a - 2
                right.append(xs[b, :, 128 * (lo + 1) : 128 * (lo + 3)])
    return jnp.dot(jnp.concatenate(left, axis=1), jnp.concatenate(right, axis=0), preferred_element_type=F32)


def shard_kernel(step, which, shard, part, weights, *refs):
    *ends, xs = refs if which == 0 else (*refs[:-3], refs[-3])
    ch = shard.shape[0] // 4 - FOLD // 4
    store_windows(xs, *rows_of([shard[...]], ch))
    pre = ends[0] if which == 0 else refs[-2]
    for pair in range(2):
        total = shard_rows(weights, which, xs, pair)
        pre[2 * pair] = part[2 * pair] + total[:, 0:128]
        pre[2 * pair + 1] = part[2 * pair + 1] + total[:, 128:256]
    if which == 1:
        finish(step, pre, *ends, refs[-1])


def rim_strips(shards, ch):
    halo = jnp.concatenate([unfold(s[0:FOLD].astype(F32), ch) for s in shards], axis=0).astype(BF16)
    own = jnp.concatenate([unfold(s[FOLD:].astype(F32), ch) for s in shards], axis=0).astype(BF16)
    return strips(halo, own)


def ordered(own, other):
    even = lax.axis_index("chan") % 2 == 0
    return [jnp.where(even, own[...], other[...]), jnp.where(even, other[...], own[...])]


def rim_drive_kernel(from_right, from_left, inp, weights, *refs):
    part, xi, inp32 = refs[-3:]
    store_input_rim(xi, *input_rows(0, inp32, inp, from_right, from_left))
    part[...] = input_part(weights, xi, 0, 128)


def rim_kernel(*refs):
    *blocks, part, hid, cell, to_right, to_left, from_right, from_left, w, hid_out, cell_out, pre = refs
    ch = cell.shape[0] // 4
    if len(blocks) == 4:
        first = lax.axis_index("chan") // 2 == 0
        here, there = ordered(*blocks[:2]), ordered(*blocks[:1:-1])
        shards = [jnp.where(first, here[k], there[k]) for k in (0, 1)]
        shards += [jnp.where(first, there[k], here[k]) for k in (0, 1)]
    else:
        shards = [blocks[0][c] for c in range(blocks[0].shape[0])]
    pre[0] = part[...] + hidden_rim(w, rim_strips(shards, ch), 0)
    h, c = rim_gates(pre, to_right, to_left, from_right, from_left, ch)
    for y in range(4):
        at = slice(y * ch, (y + 1) * ch)
        hid_out[at, :] = patch(hid[at, :].astype(F32), h, y).astype(BF16)
        cell_out[at, :] = patch(cell[at, :], c, y)
    hid_out[4 * ch : 4 * ch + FOLD, :] = rim_fold(h)


def call(kernel, outs, scratch, *args, far=0, us=1, same=None):
    return pl.pallas_call(
        kernel,
        out_shape=[jax.ShapeDtypeStruct(s, d) for s, d in outs],
        in_specs=[pl.BlockSpec(memory_space=pltpu.HBM)] * far
        + [pl.BlockSpec(memory_space=pltpu.VMEM)] * (len(args) - far),
        out_specs=[pl.BlockSpec(memory_space=pltpu.VMEM)] * len(outs),
        scratch_shapes=[pltpu.VMEM(s, d) for s, d in scratch] + ([pltpu.SemaphoreType.DMA((far,))] if far else []),
        input_output_aliases=same or {},
        cost_estimate=pl.CostEstimate(flops=int(us * 1e9), bytes_accessed=0, transcendentals=0),
        compiler_params=pltpu.CompilerParams(vmem_limit_bytes=24 << 20),
    )(*[pltpu.with_memory_space_constraint(a, pltpu.HBM) if i < far else a for i, a in enumerate(args)])


def shards(inputs, hidden_init, cell_init, w_input, w_hidden, gate_bias):
    ch, rows, cols = hidden_init.shape
    gate = 4 * ch
    depth = w_hidden.shape[3]
    cin = w_input.shape[3]
    hid = hidden_init.reshape(ch * rows, cols)
    cell = cell_init.reshape(ch * rows, cols)
    inp = inputs.reshape(-1, cols)
    wx = jnp.transpose(w_input, (0, 1, 3, 2)).reshape(25 * cin, gate)
    bias = gate_bias.reshape(1, gate)
    driven = [((gate, padded(25 * cin)), BF16), ((4, gate, 128), F32)]
    stack = ((padded(25 * cin), 512), BF16)
    inp32 = (inp.shape, F32)
    to_right, to_left, hid, weights, part = call(
        pack_kernel,
        [((FOLD + 8, 128), F32), ((FOLD + 8, 128), F32), ((4 * ch, 128), F32), *driven],
        [(hid.shape, BF16), (cell.shape, F32), (inp.shape, BF16), (wx.shape, BF16), (bias.shape, F32),
         (hid.shape, F32), inp32, stack],
        hid, cell, inp, wx, bias, far=5, us=20,
    )
    weights, driven = call(drive_kernel, driven, [inp32, stack], inp, wx, bias, weights, part, us=0.01, same={3: 0, 4: 1})
    (main,) = call(main_kernel, [((4 * ch, 128), BF16)], [], hid, us=0.01)
    n = lax.axis_size("lon")
    came_left = lax.ppermute(to_right, "lon", [(i, (i + 1) % n) for i in range(n)])
    came_right = lax.ppermute(to_left, "lon", [((i + 1) % n, i) for i in range(n)])
    from_right, from_left, strip = call(
        strip_kernel, [(to_left.shape, F32), (to_left.shape, F32), ((2 * FOLD, 128), BF16)], [],
        came_left, came_right, to_right, to_left,
    )
    shards = lax.axis_size("chan")
    paired = shards == 4 and 2 * ch == 128

    def others(x):
        return [lax.ppermute(x, "chan", [(i, i ^ k) for i in range(shards)]) for k in (1, 2)]

    def onward(same, before):
        (same,) = call(after_kernel, [(same.shape, BF16)], [], same, before, us=0.01)
        return same, lax.ppermute(same, "chan", [(i, i ^ 1) for i in range(shards)])

    field = main
    traveling = [lax.ppermute(field, "chan", [(i, i ^ k) for i in range(shards)]) for k in (1, 2, 3)] if paired else None
    blocks = [strip, *[lax.ppermute(strip, "chan", [(i, i ^ k) for i in range(shards)]) for k in (1, 2, 3)]] if paired else [lax.all_gather(strip, "chan", axis=0)]
    for step in range(STEPS):
        last = step == STEPS - 1
        hid32 = ((4 * ch, 128), F32)
        pre = ((4, gate, 128), F32)
        outs = [((4 * ch, 128), BF16), ((4 * ch, 128), F32)]
        rim = None
        if paired:
            other, same, *cross = traveling
            windowed = ((5, 2 * ch, 768), BF16)
            (part,) = call(near_kernel, [pre], [windowed], field, other, driven, w_hidden, us=0.01)
            if cross:
                (cross,) = cross
            else:
                (split,) = call(
                    split_kernel, [((2, 5 * len(SETS), gate, 128), BF16)], [], w_hidden, part, us=0.01
                )
                same, cross = onward(same, split)
        if not last:
            rim = call(
                rim_drive_kernel, [((gate, 128), F32)], [((padded(25 * cin), 128), BF16), inp32],
                from_right, from_left, inp, weights, *([part] if paired else []), us=0.01,
            )
        if paired and last:
            (part,) = call(
                functools.partial(shard_kernel, step, 0), [pre], [((5, ch, 768), BF16)],
                same, part, split, us=0.01,
            )
            field, cell = call(
                functools.partial(shard_kernel, step, 1), outs, [((5, ch, 768), BF16), pre, hid32],
                cross, part, split, cell, us=0.01,
            )
        elif paired:
            field, cell = call(
                functools.partial(far_kernel, step), outs, [windowed, pre, hid32],
                cross, same, part, cell, w_hidden, *(rim or []), us=0.01,
            )
        else:
            gathered = lax.all_gather(field, "chan", axis=0)
            field, cell = call(
                functools.partial(whole_kernel, step), outs,
                [((5, depth, 768), BF16), pre, hid32], gathered, driven, cell, w_hidden, us=3,
            )
        if not last:
            field, cell = call(
                rim_kernel, [((4 * ch + FOLD, 128), BF16), ((4 * ch, 128), F32)], [((1, gate, 128), F32)],
                *blocks[:2], *blocks[:1:-1], *rim, field, cell,
                to_right, to_left, from_right, from_left, w_hidden, us=0.01,
            )
            traveling = others(field) if paired else None
            (driven,) = call(
                functools.partial(next_drive_kernel, step + 1), [pre], [stack, inp32],
                from_right, from_left, inp, weights, field, us=0.01,
            )
    return field.reshape(ch, rows, cols), cell.reshape(ch, rows, cols)


def solution(mesh):
    in_specs = (
        P(None, None, "groups", "lon"),
        P("chan", "groups", "lon"),
        P("chan", "groups", "lon"),
        P(None, None, "chan", None),
        P(None, None, "chan", None),
        P("chan"),
    )
    out_specs = (P("chan", "groups", "lon"), P("chan", "groups", "lon"))
    return jax.shard_map(shards, mesh=mesh, in_specs=in_specs, out_specs=out_specs, check_vma=False)
```
